128 devices in a mesh: train: 16 (over y, z), val: 8 (over x, core).
Axes of the slice: x: 4, y: 4, z: 4, core: 2. Of those that a mesh axis runs over, the one named last changes fastest.
Arguments:
- train_embed: bfloat16 [49152, 2048], P('train'), may hold values from -6 to 6
- val_embed: bfloat16 [8192, 2048], P('val', 'train'), may hold values from -6 to 6
- train_labels: int32 [49152], P('train'), may hold values from 0 to 9
- val_labels: int32 [8192], P('val'), may hold values from 0 to 9
- label_cost: float32 [10, 10], replicated, may hold values from 0.05 to 0.4
Outputs:
- train_potential: float32 [49152], P('train')
- val_potential: float32 [8192], P('val')
The draws below stay inside these ranges and needn't reach their ends.
All inputs are finite; a program needn't handle non-finite values.
Results may differ from the reference program's by a relative error of at most 0.0003.
Values may be sent and summed in bfloat16 or wider, within the bound.
No kernel may reach another device: no remote copies, remote signals or barrier semaphores. Data moves between devices by JAX's collectives and lax.ppermute only.
A program may use at most 128 MiB of HBM per device.

```python
import math
import jax
import jax.numpy as jnp
from jax import lax

D = 2048
NCLS = 10
R_DEV = 3072
ITERS = 3
NT = 49152
NV = 8192
N_TRAIN = 16


def shared_rows(key):
    return jnp.clip(jax.random.normal(key, (NV, D), jnp.float32), -6.0, 6.0)


def widen_rows(values):
    far_rows = jnp.arange(8, dtype=jnp.int32) * (NV // 8)
    return values.at[far_rows].set(values[far_rows] * 2.0)


def draw_val_embed(key, part):
    base = shared_rows(key)
    base = widen_rows(base)
    return jnp.clip(base, -6.0, 6.0).astype(jnp.bfloat16)


def draw_train_embed(key, part):
    key = jax.random.fold_in(key, 5)
    values = jax.random.normal(key, (NT, D), jnp.float32)
    return jnp.clip(values, -6.0, 6.0).astype(jnp.bfloat16)


def with_ends(array, rng, smallest, high):
    index_at = [jax.random.randint(jax.random.fold_in(rng, axis), (), 0, length) for axis, length in enumerate(array.shape)]
    main_axis = array.shape.index(max(array.shape))
    neighbour = index_at[:main_axis] + [(index_at[main_axis] + 1) % array.shape[main_axis]] + index_at[main_axis + 1:]
    return array.at[tuple(index_at)].set(smallest).at[tuple(neighbour)].set(high)


def setup_inputs(seed: int = 0) -> dict:
    key_of = jax.random.split(jax.random.key(seed), 6)
    train_embed = draw_train_embed(jax.random.fold_in(key_of[5], 71), 0)
    val_embed = draw_val_embed(jax.random.fold_in(key_of[5], 71), 0)
    train_labels = with_ends(jax.random.randint(key_of[2], (NT,), 0, NCLS), jax.random.fold_in(key_of[2], 1), 0, NCLS - 1).astype(jnp.int32)
    val_labels = with_ends(jax.random.randint(key_of[3], (NV,), 0, NCLS), jax.random.fold_in(key_of[3], 1), 0, NCLS - 1).astype(jnp.int32)
    label_cost = jnp.clip(jax.random.uniform(key_of[4], (NCLS, NCLS), jnp.float32, 0.05, 0.4), 0.05, 0.4)
    return {"train_embed": train_embed, "val_embed": val_embed, "train_labels": train_labels, "val_labels": val_labels, "label_cost": label_cost}


entropic_reg = 0.01


def make_cost(embed_rows, row_sq, row_labels, val_embed, val_sq, val_labels, label_cost):
    product = jnp.dot(embed_rows, val_embed.T, preferred_element_type=jnp.float32)
    label_part = label_cost[row_labels][:, val_labels]
    return (row_sq[:, None] + val_sq[None, :] - 2.0 * product) / D + label_part


def reference(train_embed, val_embed, train_labels, val_labels, label_cost):
    train_sq = jnp.sum(jnp.square(train_embed.astype(jnp.float32)), axis=1)
    val_sq = jnp.sum(jnp.square(val_embed.astype(jnp.float32)), axis=1)
    embed_blocks = train_embed.reshape(N_TRAIN, R_DEV, D)
    sq_blocks = train_sq.reshape(N_TRAIN, R_DEV)
    label_blocks = train_labels.reshape(N_TRAIN, R_DEV)
    val_potential = jnp.zeros((NV,), jnp.float32)
    train_potential = jnp.zeros((NT,), jnp.float32)
    for sweep in range(ITERS):
        def row_block(pieces):
            embed_rows, row_sq, row_labels = pieces
            cost = make_cost(embed_rows, row_sq, row_labels, val_embed, val_sq, val_labels, label_cost)
            scores = (val_potential[None, :] - cost) / entropic_reg
            peak = jnp.max(scores, axis=1)
            summed = jnp.sum(jnp.exp(scores - peak[:, None]), axis=1)
            return -entropic_reg * (peak + jnp.log(summed) - math.log(NV))

        train_potential = lax.map(row_block, (embed_blocks, sq_blocks, label_blocks)).reshape(NT)
        pot_blocks = train_potential.reshape(N_TRAIN, R_DEV)

        def col_block(running, pieces):
            peak, summed = running
            embed_rows, row_sq, row_labels, row_pot = pieces
            cost = make_cost(embed_rows, row_sq, row_labels, val_embed, val_sq, val_labels, label_cost)
            scores = (row_pot[:, None] - cost) / entropic_reg
            new_peak = jnp.maximum(peak, jnp.max(scores, axis=0))
            summed = summed * jnp.exp(peak - new_peak) + jnp.sum(jnp.exp(scores - new_peak[None, :]), axis=0)
            return (new_peak, summed), None

        start_state = (jnp.full((NV,), -jnp.inf, jnp.float32), jnp.zeros((NV,), jnp.float32))
        (peak, summed), unused = lax.scan(col_block, start_state, (embed_blocks, sq_blocks, label_blocks, pot_blocks))
        val_potential = -entropic_reg * (peak + jnp.log(summed) - math.log(NT))
    return train_potential, val_potential
```

```python
import math

import jax
import jax.numpy as jnp
from jax import lax
from jax.experimental import pallas as pl
from jax.experimental.pallas import tpu as pltpu
from jax.sharding import PartitionSpec as P

EPS = 0.01
LOG2E = math.log2(math.e)
KAPPA = LOG2E / EPS
VMEM = pl.BlockSpec(memory_space=pltpu.VMEM)
HBM = pl.BlockSpec(memory_space=pltpu.HBM)
LAST = (((1,), (1,)), ((), ()))
SPLITS = 16
SMALL = 10
SIDE = 4


def params(mib):
    return pltpu.CompilerParams(vmem_limit_bytes=mib << 20)


def in_vmem(x):
    return pltpu.with_memory_space_constraint(x, pltpu.VMEM)


def in_hbm(x):
    return pltpu.with_memory_space_constraint(x, pltpu.HBM)


def shape_of(shape, dtype=jnp.float32):
    return jax.ShapeDtypeStruct(shape, dtype)


def split_rows(x):
    n = x.shape[1]
    row = lax.broadcasted_iota(jnp.int32, (SPLITS, n), 0)
    hi = x.astype(jnp.bfloat16).astype(jnp.float32)
    mid = (x - hi).astype(jnp.bfloat16).astype(jnp.float32)
    low = x - hi - mid
    parts = jnp.where(row == 0, hi, jnp.where(row == 1, mid, jnp.where(row == 2, low, 0.0)))
    return parts.astype(jnp.bfloat16)


def logsum2(rows):
    peak = rows[0]
    for r in rows[1:]:
        peak = jnp.maximum(peak, r)
    total = jnp.exp2(rows[0] - peak)
    for r in rows[1:]:
        total = total + jnp.exp2(r - peak)
    return peak + jnp.log2(total)


def turn(block):
    r = lax.broadcasted_iota(jnp.int32, (128, 128), 0)
    c = lax.broadcasted_iota(jnp.int32, (128, 128), 1)
    return jnp.sum(jnp.where(r == c, block, 0.0), axis=0, keepdims=True)


def one_hot_rows(labels, slots):
    n = labels.shape[1]
    slot = lax.broadcasted_iota(jnp.int32, (128, n), 0)
    hot = ((slot % 16 == labels) & (slot < slots)).astype(jnp.float32)
    return jnp.transpose(hot).astype(jnp.bfloat16)


def prepare_kernel(
    features, tile, label_cost, train_labels, val_labels,
    source, train, train_hot, label_rows, labels, more_labels, costs, sems, label_sems,
):
    classes = label_cost.shape[0]
    label_copies = [
        pltpu.make_async_copy(train_labels, labels, label_sems.at[0]),
        pltpu.make_async_copy(val_labels, more_labels, label_sems.at[1]),
        pltpu.make_async_copy(label_cost, costs, label_sems.at[2]),
    ]
    spans = [pl.ds(k * tile, tile) for k in range(train.shape[0] // tile)]
    copies = [
        pltpu.make_async_copy(source.at[at], train.at[at], sems.at[k]) for k, at in enumerate(spans)
    ]
    for copy in label_copies + copies:
        copy.start()
    for copy in label_copies:
        copy.wait()
    table = jnp.pad(costs[...], ((0, 16 - classes), (0, 128 - classes))) * (-0.5 * features)
    hi = table.astype(jnp.bfloat16)
    rest = table - hi.astype(jnp.float32)
    mid = rest.astype(jnp.bfloat16)
    low = (rest - mid.astype(jnp.float32)).astype(jnp.bfloat16)
    table = jnp.concatenate([hi, mid, low, jnp.zeros((80, 128), jnp.bfloat16)], axis=0)
    out = lax.dot_general(
        one_hot_rows(more_labels[...], 16), table, LAST, preferred_element_type=jnp.float32
    )
    label_rows[...] = out.astype(jnp.bfloat16)
    train_hot[...] = one_hot_rows(labels[...], 48)
    for copy in copies:
        copy.wait()


def train_kernel(tile, log_cols, source, row_pot, r0, r1, r2, r3, out, squares, buf, sems):
    rows, features = source.shape
    count, depth = rows // tile, buf.shape[0]

    def fetch(k):
        at = pl.ds(k * tile, tile)
        return pltpu.make_async_copy(source.at[at], buf.at[k % depth], sems.at[k % depth])

    for k in range(depth - 1):
        fetch(k).start()
    for k in range(count):
        if k + depth - 1 < count:
            fetch(k + depth - 1).start()
        fetch(k).wait()
        for r in range(0, tile, 64):
            total = jnp.zeros((64, 128), jnp.float32)
            for c in range(features // 128):
                piece = buf[k % depth, pl.ds(r, 64), pl.ds(c * 128, 128)].astype(jnp.float32)
                total = total + piece * piece
            squares[pl.ds(k * tile + r, 64), :] = total
    ones = jnp.ones((SPLITS, 128), jnp.bfloat16)
    rest, norm = squares[...], 0.0
    for _ in range(3):
        part = rest.astype(jnp.bfloat16)
        rest = rest - part.astype(jnp.float32)
        norm = norm + lax.dot_general(ones, part, LAST, preferred_element_type=jnp.float32)
    total = (r0[...] + r1[...]) + (r2[...] + r3[...])
    pot = (row_pot[...] + (log_cols - jnp.log2(total))) * (1.0 / KAPPA)
    out[...] = pot + norm[0:1, :] * (1.0 / features)


def part_kernel(plan, count, row, tile, alpha, *refs):
    vals, (train, *given), results = refs[:count], refs[count : count + 3], refs[count + 3 :]
    first, last = given[0].dtype == jnp.bfloat16, alpha is not None
    if first:
        label_rows, train_hot = given
    else:
        before, sq_before = given
    scores, out = results[:2]
    sq = results[2] if last else out
    rows = train.shape[0]
    half = scores.shape[0] // 2
    pieces = len(plan[0][2])
    to = pl.ds(row, half * pieces)
    t = lax.axis_index("train")
    y, z = t // SIDE, t % SIDE

    def piece(part, r, n):
        place, start = part
        return vals[place][pl.ds(start + r, n), :]

    for h in range(pieces):
        for r in range(0, half, 128):
            at = pl.ds(row + h * half + r, 128)
            total = jnp.zeros((128, 128), jnp.float32) if first else sq_before[at, :]
            for _, _, parts in plan:
                value = piece(parts[h], r, 128).astype(jnp.float32)
                total = total + value * value
            if last:
                total = jnp.sum(total, axis=1, keepdims=True) * 0.5
                sq[pl.ds(h * half + r, 128), :] = jnp.broadcast_to(total, (128, 128))
            else:
                sq[at, :] = total

    for k in range(rows // tile):
        at = pl.ds(k * tile, tile)
        left, right = [], []
        for dy, dz, parts in plan:
            left.append(jnp.concatenate([piece(part, 0, half) for part in parts], axis=0))
            block = ((y + dy) % SIDE) * SIDE + (z + dz) % SIDE
            right.append(train[at, pl.ds(pl.multiple_of(block * 128, 128), 128)])
        if first:
            left.append(label_rows[to, :])
            right.append(train_hot[at, :])
        x = lax.dot_general(
            jnp.concatenate(left, axis=1),
            jnp.concatenate(right, axis=1),
            LAST,
            preferred_element_type=jnp.float32,
        )
        if not first:
            x = x + before[to, at]
        if last:
            x = (x - jnp.concatenate([sq[...]] * (tile // 128), axis=1)) * alpha
            peak = jnp.max(x, axis=0, keepdims=True)
            total = jnp.sum(jnp.exp2(x - peak), axis=0, keepdims=True)
            out[:, at] = peak + jnp.log2(total)
        scores[to, at] = x


def product_part(name, plan, row, tile, train, given, alpha=None):
    rows = train.shape[0]
    first, last = given[0].dtype == jnp.bfloat16, alpha is not None
    cols = given[0].shape[0]
    vals = []

    def place(array):
        for k, known in enumerate(vals):
            if known is array:
                return k
        vals.append(array)
        return len(vals) - 1

    plan = [(dy, dz, [(place(v), start) for v, start in parts]) for dy, dz, parts in plan]
    out = [pltpu.VMEM((cols, rows), jnp.float32)]
    out.append(shape_of((1, rows)) if last else shape_of((cols, 128)))
    given = given if first else [in_vmem(given[0]), given[1]]
    operands = [*vals, in_vmem(train), *given]
    depth = len(plan) * 128
    height = len(plan[0][2]) * cols // 2
    return pl.pallas_call(
        lambda *refs: part_kernel(plan, len(vals), row, tile, alpha, *refs),
        out_shape=tuple(out),
        in_specs=[VMEM] * len(operands),
        out_specs=(VMEM,) * len(out),
        scratch_shapes=[pltpu.VMEM((height, 128), jnp.float32)] if last else [],
        input_output_aliases={} if first else {len(operands) - 2: 0},
        compiler_params=params(SMALL),
        cost_estimate=pl.CostEstimate(
            flops=2 * height * rows * depth, bytes_accessed=0, transcendentals=0
        ),
        name=name,
    )(*operands)


def from_step(x, dy, dz):
    pairs = [
        (y * SIDE + z, ((y - dy) % SIDE) * SIDE + (z - dz) % SIDE)
        for y in range(SIDE)
        for z in range(SIDE)
    ]
    return lax.ppermute(x, "train", pairs)


def gather(x):
    h = x.shape[0] // 2
    low = lambda v, n: (v, n * h)
    cut = lambda v, n: v[n * h : (n + 1) * h]
    z1, z3 = from_step(x, 0, 1), from_step(x, 0, 3)
    y1, y3 = from_step(x, 1, 0), from_step(x, 3, 0)
    far = from_step(y1, 1, 2)
    both = lambda v: [low(v, 0), low(v, 1)]
    near = [(0, 0, both(x)), (0, 1, both(z1)), (0, 3, both(z3)), (1, 0, both(y1)), (3, 0, both(y3))]

    first = jnp.concatenate([cut(z1, 0), cut(z3, 0)], axis=0)
    second = jnp.concatenate([cut(y1, 1), cut(y3, 1)], axis=0)
    a1, a3 = from_step(first, 1, 0), from_step(first, 3, 0)
    b1, b3 = from_step(second, 0, 1), from_step(second, 0, 3)
    diagonal = [
        (dy, dz, [low(a, i), low(b, j)])
        for j, (dy, a) in enumerate(((1, a1), (3, a3)))
        for i, (dz, b) in enumerate(((1, b1), (3, b3)))
    ]
    diagonal.append((2, 2, both(far)))

    join = lambda *v: jnp.concatenate(v, axis=0)
    az = from_step(join(cut(z1, 0), cut(a1, 0), cut(a3, 0)), 0, 1)
    bz = from_step(join(cut(z3, 1), b3), 0, 3)
    by = from_step(join(cut(y1, 1), cut(b1, 0), cut(b3, 0)), 1, 0)
    ay = from_step(join(cut(y3, 0), a3), 3, 0)
    across = [(0, 2), (1, 2), (3, 2)]
    along = [(2, 0), (2, 1), (2, 3)]
    last_a = [(*d, [low(az, k)]) for k, d in enumerate(across)]
    last_a += [(*d, [low(ay, k)]) for k, d in enumerate(along)]
    last_b = [(*d, [low(bz, k)]) for k, d in enumerate(across)]
    last_b += [(*d, [low(by, k)]) for k, d in enumerate(along)]
    return near, diagonal, last_a, last_b


def kernel_kernel(log_cols, scores, l0, l1, l2, l3, kern, row_pot, peaks, col_log, peak_b, log_b):
    cols, rows = scores.shape
    pot = log_cols - logsum2([l0[...], l1[...], l2[...], l3[...]])
    row_pot[...] = pot
    block = 64

    @pl.loop(0, cols // block, unroll=4)
    def _(k):
        part = pl.ds(pl.multiple_of(k * block, block), block)
        peak = None
        for c in range(rows // 128):
            lane = pl.ds(c * 128, 128)
            x = scores[part, lane] + row_pot[:, lane]
            peak = x if peak is None else jnp.maximum(peak, x)
        peak = jnp.max(peak, axis=1, keepdims=True)
        peak = jnp.broadcast_to(peak, (block, 128))
        total = jnp.zeros((block, 128), jnp.float32)
        for c in range(rows // 128):
            lane = pl.ds(c * 128, 128)
            e = jnp.exp2((scores[part, lane] - peak) + row_pot[:, lane])
            total = total + e
            kern[part, lane] = e.astype(kern.dtype)
        total = jnp.sum(total, axis=1, keepdims=True)
        peak_b[part, :] = peak
        log_b[part, :] = peak + jnp.log2(total)

    for k in range(cols // 128):
        part = pl.ds(k * 128, 128)
        peaks[:, part] = turn(peak_b[part, :])
        col_log[:, part] = jnp.broadcast_to(turn(log_b[part, :]), (col_log.shape[0], 128))


def first_rows_kernel(total_rows, kern, peaks, col_logs, weights, first_log, sums):
    logs = col_logs[...]
    peak = jnp.max(logs, axis=0, keepdims=True)
    whole = peak + jnp.log2(jnp.sum(jnp.exp2(logs - peak), axis=0, keepdims=True))
    first_log[...] = whole
    v = jnp.exp2(peaks[...] - whole) * total_rows
    weights[...] = v
    out = jnp.dot(split_rows(v), kern[...], preferred_element_type=jnp.float32)
    sums[...] = jnp.sum(out, axis=0, keepdims=True)


def next_rows_kernel(total_rows, kern, weights, col_sums, sums):
    v = weights[...] * (total_rows / jnp.sum(col_sums[...], axis=0, keepdims=True))
    out = jnp.dot(split_rows(v), kern[...], preferred_element_type=jnp.float32)
    sums[...] = jnp.sum(out, axis=0, keepdims=True)


def cols_kernel(total_cols, kern, weights, r0, r1, r2, r3, sums):
    u = total_cols / ((r0[...] + r1[...]) + (r2[...] + r3[...]))
    out = lax.dot_general(split_rows(u), kern[...], LAST, preferred_element_type=jnp.float32)
    out = jnp.sum(out, axis=0, keepdims=True) * weights[...]
    sums[...] = jnp.broadcast_to(out, sums.shape)


def other_chips(x):
    n = lax.axis_size("val")
    return [
        lax.ppermute(x, "val", [(i, (i + 2 * k) % n) for i in range(n)]) for k in range(1, n // 2)
    ]


def other_core(x):
    return lax.ppermute(x, "val", [(i, i ^ 1) for i in range(lax.axis_size("val"))])


def spread(x):
    n = lax.axis_size("train")
    return lax.all_to_all(x.reshape(n, 1, -1), "train", 0, 0).reshape(n, -1)


def shards(train_embed, val_embed, train_labels, val_labels, label_cost):
    rows, features = train_embed.shape
    cols = val_embed.shape[0]
    groups = lax.axis_size("train")
    total_rows = float(rows * groups)
    total_cols = float(cols * lax.axis_size("val"))
    vec_r, vec_c = shape_of((1, rows)), shape_of((1, cols))

    near, diagonal, last_a, last_b = gather(val_embed)
    train, train_hot, label_rows = pl.pallas_call(
        lambda *refs: prepare_kernel(features, 512, *refs),
        out_shape=(
            pltpu.VMEM((rows, features), jnp.bfloat16),
            shape_of((rows, 128), jnp.bfloat16),
            shape_of((cols, 128), jnp.bfloat16),
        ),
        in_specs=[HBM] * 4,
        out_specs=(VMEM,) * 3,
        scratch_shapes=[
            pltpu.VMEM((1, rows), jnp.int32),
            pltpu.VMEM((1, cols), jnp.int32),
            pltpu.VMEM(label_cost.shape, jnp.float32),
            pltpu.SemaphoreType.DMA((rows // 512,)),
            pltpu.SemaphoreType.DMA((3,)),
        ],
        compiler_params=params(SMALL),
        name="prepare",
    )(
        in_hbm(label_cost),
        in_hbm(train_labels.reshape(1, rows)),
        in_hbm(val_labels.reshape(1, cols)),
        in_hbm(train_embed),
    )
    alpha = 2.0 * KAPPA / features
    given = product_part("product_near", near, 0, 1024, train, [label_rows, train_hot])
    scores, squares = product_part("product_diagonal", diagonal, 0, 1024, train, given)
    scores, log_a = product_part("product_a", last_a, 0, 1024, train, [scores, squares], alpha)
    scores, log_b = product_part(
        "product_b", last_b, cols // 2, 1024, train, [scores, squares], alpha
    )
    row_log = jnp.logaddexp2(log_a, log_b)

    both = jnp.logaddexp2(row_log, other_core(row_log))
    kern, row_pot, peaks, col_log = pl.pallas_call(
        lambda *refs: kernel_kernel(math.log2(total_cols), *refs),
        out_shape=(shape_of((cols, rows), jnp.bfloat16), vec_r, vec_c, shape_of((groups, cols))),
        in_specs=[VMEM] * 5,
        out_specs=(VMEM,) * 4,
        scratch_shapes=[pltpu.VMEM((cols, 128), jnp.float32)] * 2,
        compiler_params=params(SMALL),
        name="kernel_matrix",
    )(scores, both, *other_chips(both))

    weights, first_log, sums = pl.pallas_call(
        lambda *refs: first_rows_kernel(total_rows, *refs),
        out_shape=(vec_c, vec_c, vec_r),
        in_specs=[VMEM] * 3,
        out_specs=(VMEM,) * 3,
        compiler_params=params(SMALL),
        name="first_rows",
    )(kern, peaks, spread(col_log))

    for sweep in range(2):
        both = sums + other_core(sums)
        others = other_chips(both)
        col_sums = pl.pallas_call(
            lambda *refs: cols_kernel(total_cols, *refs),
            out_shape=shape_of((groups, cols)),
            in_specs=[VMEM] * 6,
            out_specs=VMEM,
            compiler_params=params(SMALL),
            name="columns",
        )(kern, weights, both, *others)
        col_sums = spread(col_sums)
        if sweep == 0:
            sums = pl.pallas_call(
                lambda *refs: next_rows_kernel(total_rows, *refs),
                out_shape=vec_r,
                in_specs=[VMEM] * 3,
                out_specs=VMEM,
                compiler_params=params(SMALL),
                name="rows",
            )(kern, weights, col_sums)

    train_potential = pl.pallas_call(
        lambda *refs: train_kernel(256, math.log2(total_cols), *refs),
        out_shape=vec_r,
        in_specs=[HBM] + [VMEM] * 5,
        out_specs=VMEM,
        scratch_shapes=[
            pltpu.VMEM((rows, 128), jnp.float32),
            pltpu.VMEM((7, 256, features), jnp.bfloat16),
            pltpu.SemaphoreType.DMA((7,)),
        ],
        compiler_params=params(14),
        name="train_potential",
    )(in_hbm(train_embed), row_pot, both, *others).reshape(rows)
    col_total = jnp.sum(col_sums, axis=0, keepdims=True)
    val_potential = ((2.0 * math.log2(total_rows) - first_log) - jnp.log2(col_total)) / KAPPA
    return train_potential, val_potential.reshape(cols)


def solution(mesh):
    return jax.shard_map(
        shards,
        mesh=mesh,
        in_specs=(P("train", None), P("val", "train"), P("train"), P("val"), P()),
        out_specs=(P("train"), P("val")),
        check_vma=False,
    )
```

```python
import math

import jax
import jax.numpy as jnp
from jax import lax
from jax.experimental import pallas as pl
from jax.experimental.pallas import tpu as pltpu
from jax.sharding import PartitionSpec as P

EPS = 0.01
LOG2E = math.log2(math.e)
KAPPA = LOG2E / EPS
VMEM = pl.BlockSpec(memory_space=pltpu.VMEM)
HBM = pl.BlockSpec(memory_space=pltpu.HBM)
LAST = (((1,), (1,)), ((), ()))
SPLITS = 16
SMALL = 10
SIDE = 4


def params(mib):
    return pltpu.CompilerParams(vmem_limit_bytes=mib << 20)


def in_vmem(x):
    return pltpu.with_memory_space_constraint(x, pltpu.VMEM)


def in_hbm(x):
    return pltpu.with_memory_space_constraint(x, pltpu.HBM)


def shape_of(shape, dtype=jnp.float32):
    return jax.ShapeDtypeStruct(shape, dtype)


def split_rows(x):
    n = x.shape[1]
    row = lax.broadcasted_iota(jnp.int32, (SPLITS, n), 0)
    hi = x.astype(jnp.bfloat16).astype(jnp.float32)
    mid = (x - hi).astype(jnp.bfloat16).astype(jnp.float32)
    low = x - hi - mid
    parts = jnp.where(row == 0, hi, jnp.where(row == 1, mid, jnp.where(row == 2, low, 0.0)))
    return parts.astype(jnp.bfloat16)


def logsum2(rows):
    peak = rows[0]
    for r in rows[1:]:
        peak = jnp.maximum(peak, r)
    total = jnp.exp2(rows[0] - peak)
    for r in rows[1:]:
        total = total + jnp.exp2(r - peak)
    return peak + jnp.log2(total)


def turn(block):
    r = lax.broadcasted_iota(jnp.int32, (128, 128), 0)
    c = lax.broadcasted_iota(jnp.int32, (128, 128), 1)
    return jnp.sum(jnp.where(r == c, block, 0.0), axis=0, keepdims=True)


def one_hot_rows(labels, slots):
    n = labels.shape[1]
    slot = lax.broadcasted_iota(jnp.int32, (128, n), 0)
    hot = ((slot % 16 == labels) & (slot < slots)).astype(jnp.float32)
    return jnp.transpose(hot).astype(jnp.bfloat16)


def prepare_kernel(
    features, tile, label_cost, train_labels, val_labels,
    source, train, train_hot, label_rows, labels, more_labels, costs, sems, label_sems,
):
    classes = label_cost.shape[0]
    label_copies = [
        pltpu.make_async_copy(train_labels, labels, label_sems.at[0]),
        pltpu.make_async_copy(val_labels, more_labels, label_sems.at[1]),
        pltpu.make_async_copy(label_cost, costs, label_sems.at[2]),
    ]
    spans = [pl.ds(k * tile, tile) for k in range(train.shape[0] // tile)]
    copies = [
        pltpu.make_async_copy(source.at[at], train.at[at], sems.at[k]) for k, at in enumerate(spans)
    ]
    for copy in label_copies + copies:
        copy.start()
    for copy in label_copies:
        copy.wait()
    table = jnp.pad(costs[...], ((0, 16 - classes), (0, 128 - classes))) * (-0.5 * features)
    hi = table.astype(jnp.bfloat16)
    rest = table - hi.astype(jnp.float32)
    mid = rest.astype(jnp.bfloat16)
    low = (rest - mid.astype(jnp.float32)).astype(jnp.bfloat16)
    table = jnp.concatenate([hi, mid, low, jnp.zeros((80, 128), jnp.bfloat16)], axis=0)
    out = lax.dot_general(
        one_hot_rows(more_labels[...], 16), table, LAST, preferred_element_type=jnp.float32
    )
    label_rows[...] = out.astype(jnp.bfloat16)
    train_hot[...] = one_hot_rows(labels[...], 48)
    for copy in copies:
        copy.wait()


def train_kernel(tile, log_cols, source, row_pot, r0, r1, r2, r3, out, squares, buf, sems):
    rows, features = source.shape
    count, depth = rows // tile, buf.shape[0]

    def fetch(k):
        at = pl.ds(k * tile, tile)
        slot = lax.rem(k, depth)
        return pltpu.make_async_copy(source.at[at], buf.at[slot], sems.at[slot])

    for k in range(depth - 1):
        fetch(k).start()
    @pl.loop(0, count)
    def _(k):
        @pl.when(k + depth - 1 < count)
        def _():
            fetch(k + depth - 1).start()

        fetch(k).wait()
        for r in range(0, tile, 64):
            total = jnp.zeros((64, 128), jnp.float32)
            for c in range(features // 128):
                piece = buf[lax.rem(k, depth), pl.ds(r, 64), pl.ds(c * 128, 128)].astype(jnp.float32)
                total = total + piece * piece
            squares[pl.ds(pl.multiple_of(k * tile + r, 64), 64), :] = total
    ones = jnp.ones((SPLITS, 128), jnp.bfloat16)
    rest, norm = squares[...], 0.0
    for _ in range(3):
        part = rest.astype(jnp.bfloat16)
        rest = rest - part.astype(jnp.float32)
        norm = norm + lax.dot_general(ones, part, LAST, preferred_element_type=jnp.float32)
    total = (r0[...] + r1[...]) + (r2[...] + r3[...])
    pot = (row_pot[...] + (log_cols - jnp.log2(total))) * (1.0 / KAPPA)
    out[...] = pot + norm[0:1, :] * (1.0 / features)


def part_kernel(plan, count, row, tile, alpha, *refs):
    vals, (train, *given), results = refs[:count], refs[count : count + 3], refs[count + 3 :]
    first, last = given[0].dtype == jnp.bfloat16, alpha is not None
    if first:
        label_rows, train_hot = given
    else:
        before, sq_before = given
    scores, out = results[:2]
    sq = results[2] if last else out
    rows = train.shape[0]
    half = scores.shape[0] // 2
    pieces = len(plan[0][2])
    to = pl.ds(row, half * pieces)
    t = lax.axis_index("train")
    y, z = t // SIDE, t % SIDE

    def piece(part, r, n):
        place, start = part
        return vals[place][pl.ds(start + r, n), :]

    for h in range(pieces):
        for r in range(0, half, 128):
            at = pl.ds(row + h * half + r, 128)
            total = jnp.zeros((128, 128), jnp.float32) if first else sq_before[at, :]
            for _, _, parts in plan:
                value = piece(parts[h], r, 128).astype(jnp.float32)
                total = total + value * value
            if last:
                total = jnp.sum(total, axis=1, keepdims=True) * 0.5
                sq[pl.ds(h * half + r, 128), :] = jnp.broadcast_to(total, (128, 128))
            else:
                sq[at, :] = total

    @pl.loop(0, rows // tile)
    def _(k):
        at = pl.ds(pl.multiple_of(k * tile, tile), tile)
        left, right = [], []
        for dy, dz, parts in plan:
            left.append(jnp.concatenate([piece(part, 0, half) for part in parts], axis=0))
            block = ((y + dy) % SIDE) * SIDE + (z + dz) % SIDE
            right.append(train[at, pl.ds(pl.multiple_of(block * 128, 128), 128)])
        if first:
            left.append(label_rows[to, :])
            right.append(train_hot[at, :])
        x = lax.dot_general(
            jnp.concatenate(left, axis=1),
            jnp.concatenate(right, axis=1),
            LAST,
            preferred_element_type=jnp.float32,
        )
        if not first:
            x = x + before[to, at]
        if last:
            x = (x - jnp.concatenate([sq[...]] * (tile // 128), axis=1)) * alpha
            peak = jnp.max(x, axis=0, keepdims=True)
            total = jnp.sum(jnp.exp2(x - peak), axis=0, keepdims=True)
            out[:, at] = peak + jnp.log2(total)
        scores[to, at] = x


def product_part(name, plan, row, tile, train, given, alpha=None):
    rows = train.shape[0]
    first, last = given[0].dtype == jnp.bfloat16, alpha is not None
    cols = given[0].shape[0]
    vals = []

    def place(array):
        for k, known in enumerate(vals):
            if known is array:
                return k
        vals.append(array)
        return len(vals) - 1

    plan = [(dy, dz, [(place(v), start) for v, start in parts]) for dy, dz, parts in plan]
    out = [pltpu.VMEM((cols, rows), jnp.float32)]
    out.append(shape_of((1, rows)) if last else shape_of((cols, 128)))
    given = given if first else [in_vmem(given[0]), given[1]]
    operands = [*vals, in_vmem(train), *given]
    depth = len(plan) * 128
    height = len(plan[0][2]) * cols // 2
    return pl.pallas_call(
        lambda *refs: part_kernel(plan, len(vals), row, tile, alpha, *refs),
        out_shape=tuple(out),
        in_specs=[VMEM] * len(operands),
        out_specs=(VMEM,) * len(out),
        scratch_shapes=[pltpu.VMEM((height, 128), jnp.float32)] if last else [],
        input_output_aliases={} if first else {len(operands) - 2: 0},
        compiler_params=params(SMALL),
        cost_estimate=pl.CostEstimate(
            flops=2 * height * rows * depth, bytes_accessed=0, transcendentals=0
        ),
        name=name,
    )(*operands)


def from_step(x, dy, dz):
    pairs = [
        (y * SIDE + z, ((y - dy) % SIDE) * SIDE + (z - dz) % SIDE)
        for y in range(SIDE)
        for z in range(SIDE)
    ]
    return lax.ppermute(x, "train", pairs)


def gather(x):
    h = x.shape[0] // 2
    low = lambda v, n: (v, n * h)
    cut = lambda v, n: v[n * h : (n + 1) * h]
    z1, z3 = from_step(x, 0, 1), from_step(x, 0, 3)
    y1, y3 = from_step(x, 1, 0), from_step(x, 3, 0)
    far = from_step(y1, 1, 2)
    both = lambda v: [low(v, 0), low(v, 1)]
    near = [(0, 0, both(x)), (0, 1, both(z1)), (0, 3, both(z3)), (1, 0, both(y1)), (3, 0, both(y3))]

    first = jnp.concatenate([cut(z1, 0), cut(z3, 0)], axis=0)
    second = jnp.concatenate([cut(y1, 1), cut(y3, 1)], axis=0)
    a1, a3 = from_step(first, 1, 0), from_step(first, 3, 0)
    b1, b3 = from_step(second, 0, 1), from_step(second, 0, 3)
    diagonal = [
        (dy, dz, [low(a, i), low(b, j)])
        for j, (dy, a) in enumerate(((1, a1), (3, a3)))
        for i, (dz, b) in enumerate(((1, b1), (3, b3)))
    ]
    diagonal.append((2, 2, both(far)))

    join = lambda *v: jnp.concatenate(v, axis=0)
    az = from_step(join(cut(z1, 0), cut(a1, 0), cut(a3, 0)), 0, 1)
    bz = from_step(join(cut(z3, 1), b3), 0, 3)
    by = from_step(join(cut(y1, 1), cut(b1, 0), cut(b3, 0)), 1, 0)
    ay = from_step(join(cut(y3, 0), a3), 3, 0)
    across = [(0, 2), (1, 2), (3, 2)]
    along = [(2, 0), (2, 1), (2, 3)]
    last_a = [(*d, [low(az, k)]) for k, d in enumerate(across)]
    last_a += [(*d, [low(ay, k)]) for k, d in enumerate(along)]
    last_b = [(*d, [low(bz, k)]) for k, d in enumerate(across)]
    last_b += [(*d, [low(by, k)]) for k, d in enumerate(along)]
    return near, diagonal, last_a, last_b


def kernel_kernel(log_cols, scores, l0, l1, l2, l3, kern, row_pot, peaks, col_log, peak_b, log_b):
    cols, rows = scores.shape
    pot = log_cols - logsum2([l0[...], l1[...], l2[...], l3[...]])
    row_pot[...] = pot
    block = 64

    @pl.loop(0, cols // block, unroll=4)
    def _(k):
        part = pl.ds(pl.multiple_of(k * block, block), block)
        peak = None
        for c in range(rows // 128):
            lane = pl.ds(c * 128, 128)
            x = scores[part, lane] + row_pot[:, lane]
            peak = x if peak is None else jnp.maximum(peak, x)
        peak = jnp.max(peak, axis=1, keepdims=True)
        peak = jnp.broadcast_to(peak, (block, 128))
        total = jnp.zeros((block, 128), jnp.float32)
        for c in range(rows // 128):
            lane = pl.ds(c * 128, 128)
            e = jnp.exp2((scores[part, lane] - peak) + row_pot[:, lane])
            total = total + e
            kern[part, lane] = e.astype(kern.dtype)
        total = jnp.sum(total, axis=1, keepdims=True)
        peak_b[part, :] = peak
        log_b[part, :] = peak + jnp.log2(total)

    for k in range(cols // 128):
        part = pl.ds(k * 128, 128)
        peaks[:, part] = turn(peak_b[part, :])
        col_log[:, part] = jnp.broadcast_to(turn(log_b[part, :]), (col_log.shape[0], 128))


def first_rows_kernel(total_rows, kern, peaks, col_logs, weights, first_log, sums):
    logs = col_logs[...]
    peak = jnp.max(logs, axis=0, keepdims=True)
    whole = peak + jnp.log2(jnp.sum(jnp.exp2(logs - peak), axis=0, keepdims=True))
    first_log[...] = whole
    v = jnp.exp2(peaks[...] - whole) * total_rows
    weights[...] = v
    out = jnp.dot(split_rows(v), kern[...], preferred_element_type=jnp.float32)
    sums[...] = jnp.sum(out, axis=0, keepdims=True)


def next_rows_kernel(total_rows, kern, weights, col_sums, sums):
    v = weights[...] * (total_rows / jnp.sum(col_sums[...], axis=0, keepdims=True))
    out = jnp.dot(split_rows(v), kern[...], preferred_element_type=jnp.float32)
    sums[...] = jnp.sum(out, axis=0, keepdims=True)


def cols_kernel(total_cols, kern, weights, r0, r1, r2, r3, sums):
    u = total_cols / ((r0[...] + r1[...]) + (r2[...] + r3[...]))
    out = lax.dot_general(split_rows(u), kern[...], LAST, preferred_element_type=jnp.float32)
    out = jnp.sum(out, axis=0, keepdims=True) * weights[...]
    sums[...] = jnp.broadcast_to(out, sums.shape)


def other_chips(x):
    n = lax.axis_size("val")
    return [
        lax.ppermute(x, "val", [(i, (i + 2 * k) % n) for i in range(n)]) for k in range(1, n // 2)
    ]


def other_core(x):
    return lax.ppermute(x, "val", [(i, i ^ 1) for i in range(lax.axis_size("val"))])


def spread(x):
    n = lax.axis_size("train")
    return lax.all_to_all(x.reshape(n, 1, -1), "train", 0, 0).reshape(n, -1)


def shards(train_embed, val_embed, train_labels, val_labels, label_cost):
    rows, features = train_embed.shape
    cols = val_embed.shape[0]
    groups = lax.axis_size("train")
    total_rows = float(rows * groups)
    total_cols = float(cols * lax.axis_size("val"))
    vec_r, vec_c = shape_of((1, rows)), shape_of((1, cols))

    near, diagonal, last_a, last_b = gather(val_embed)
    train, train_hot, label_rows = pl.pallas_call(
        lambda *refs: prepare_kernel(features, 512, *refs),
        out_shape=(
            pltpu.VMEM((rows, features), jnp.bfloat16),
            shape_of((rows, 128), jnp.bfloat16),
            shape_of((cols, 128), jnp.bfloat16),
        ),
        in_specs=[HBM] * 4,
        out_specs=(VMEM,) * 3,
        scratch_shapes=[
            pltpu.VMEM((1, rows), jnp.int32),
            pltpu.VMEM((1, cols), jnp.int32),
            pltpu.VMEM(label_cost.shape, jnp.float32),
            pltpu.SemaphoreType.DMA((rows // 512,)),
            pltpu.SemaphoreType.DMA((3,)),
        ],
        compiler_params=params(SMALL),
        name="prepare",
    )(
        in_hbm(label_cost),
        in_hbm(train_labels.reshape(1, rows)),
        in_hbm(val_labels.reshape(1, cols)),
        in_hbm(train_embed),
    )
    alpha = 2.0 * KAPPA / features
    given = product_part("product_near", near, 0, 1024, train, [label_rows, train_hot])
    scores, squares = product_part("product_diagonal", diagonal, 0, 1024, train, given)
    scores, log_a = product_part("product_a", last_a, 0, 1024, train, [scores, squares], alpha)
    scores, log_b = product_part(
        "product_b", last_b, cols // 2, 1024, train, [scores, squares], alpha
    )
    row_log = jnp.logaddexp2(log_a, log_b)

    both = jnp.logaddexp2(row_log, other_core(row_log))
    kern, row_pot, peaks, col_log = pl.pallas_call(
        lambda *refs: kernel_kernel(math.log2(total_cols), *refs),
        out_shape=(shape_of((cols, rows), jnp.bfloat16), vec_r, vec_c, shape_of((groups, cols))),
        in_specs=[VMEM] * 5,
        out_specs=(VMEM,) * 4,
        scratch_shapes=[pltpu.VMEM((cols, 128), jnp.float32)] * 2,
        compiler_params=params(SMALL),
        name="kernel_matrix",
    )(scores, both, *other_chips(both))

    weights, first_log, sums = pl.pallas_call(
        lambda *refs: first_rows_kernel(total_rows, *refs),
        out_shape=(vec_c, vec_c, vec_r),
        in_specs=[VMEM] * 3,
        out_specs=(VMEM,) * 3,
        compiler_params=params(SMALL),
        name="first_rows",
    )(kern, peaks, spread(col_log))

    for sweep in range(2):
        both = sums + other_core(sums)
        others = other_chips(both)
        col_sums = pl.pallas_call(
            lambda *refs: cols_kernel(total_cols, *refs),
            out_shape=shape_of((groups, cols)),
            in_specs=[VMEM] * 6,
            out_specs=VMEM,
            compiler_params=params(SMALL),
            name="columns",
        )(kern, weights, both, *others)
        col_sums = spread(col_sums)
        if sweep == 0:
            sums = pl.pallas_call(
                lambda *refs: next_rows_kernel(total_rows, *refs),
                out_shape=vec_r,
                in_specs=[VMEM] * 3,
                out_specs=VMEM,
                compiler_params=params(SMALL),
                name="rows",
            )(kern, weights, col_sums)

    train_potential = pl.pallas_call(
        lambda *refs: train_kernel(256, math.log2(total_cols), *refs),
        out_shape=vec_r,
        in_specs=[HBM] + [VMEM] * 5,
        out_specs=VMEM,
        scratch_shapes=[
            pltpu.VMEM((rows, 128), jnp.float32),
            pltpu.VMEM((7, 256, features), jnp.bfloat16),
            pltpu.SemaphoreType.DMA((7,)),
        ],
        compiler_params=params(14),
        name="train_potential",
    )(in_hbm(train_embed), row_pot, both, *others).reshape(rows)
    col_total = jnp.sum(col_sums, axis=0, keepdims=True)
    val_potential = ((2.0 * math.log2(total_rows) - first_log) - jnp.log2(col_total)) / KAPPA
    return train_potential, val_potential.reshape(cols)


def solution(mesh):
    return jax.shard_map(
        shards,
        mesh=mesh,
        in_specs=(P("train", None), P("val", "train"), P("train"), P("val"), P()),
        out_specs=(P("train"), P("val")),
        check_vma=False,
    )
```

```python
import math

import jax
import jax.numpy as jnp
from jax import lax
from jax.experimental import pallas as pl
from jax.experimental.pallas import tpu as pltpu
from jax.sharding import PartitionSpec as P

EPS = 0.01
LOG2E = math.log2(math.e)
KAPPA = LOG2E / EPS
VMEM = pl.BlockSpec(memory_space=pltpu.VMEM)
HBM = pl.BlockSpec(memory_space=pltpu.HBM)
LAST = (((1,), (1,)), ((), ()))
SPLITS = 16
SMALL = 10
SIDE = 4


def params(mib):
    return pltpu.CompilerParams(vmem_limit_bytes=mib << 20)


def in_vmem(x):
    return pltpu.with_memory_space_constraint(x, pltpu.VMEM)


def in_hbm(x):
    return pltpu.with_memory_space_constraint(x, pltpu.HBM)


def shape_of(shape, dtype=jnp.float32):
    return jax.ShapeDtypeStruct(shape, dtype)


def split_rows(x):
    n = x.shape[1]
    row = lax.broadcasted_iota(jnp.int32, (SPLITS, n), 0)
    hi = x.astype(jnp.bfloat16).astype(jnp.float32)
    mid = (x - hi).astype(jnp.bfloat16).astype(jnp.float32)
    low = x - hi - mid
    parts = jnp.where(row == 0, hi, jnp.where(row == 1, mid, jnp.where(row == 2, low, 0.0)))
    return parts.astype(jnp.bfloat16)


def logsum2(rows):
    peak = rows[0]
    for r in rows[1:]:
        peak = jnp.maximum(peak, r)
    total = jnp.exp2(rows[0] - peak)
    for r in rows[1:]:
        total = total + jnp.exp2(r - peak)
    return peak + jnp.log2(total)


def turn(block):
    r = lax.broadcasted_iota(jnp.int32, (128, 128), 0)
    c = lax.broadcasted_iota(jnp.int32, (128, 128), 1)
    return jnp.sum(jnp.where(r == c, block, 0.0), axis=0, keepdims=True)


def one_hot_rows(labels, slots):
    n = labels.shape[1]
    slot = lax.broadcasted_iota(jnp.int32, (128, n), 0)
    hot = ((slot % 16 == labels) & (slot < slots)).astype(jnp.float32)
    return jnp.transpose(hot).astype(jnp.bfloat16)


def prepare_kernel(
    features, tile, label_cost, train_labels, val_labels,
    source, train, train_hot, label_rows, labels, more_labels, costs, sems, label_sems,
):
    classes = label_cost.shape[0]
    label_copies = [
        pltpu.make_async_copy(train_labels, labels, label_sems.at[0]),
        pltpu.make_async_copy(val_labels, more_labels, label_sems.at[1]),
        pltpu.make_async_copy(label_cost, costs, label_sems.at[2]),
    ]
    spans = [pl.ds(k * tile, tile) for k in range(train.shape[0] // tile)]
    copies = [
        pltpu.make_async_copy(source.at[at], train.at[at], sems.at[k]) for k, at in enumerate(spans)
    ]
    for copy in label_copies + copies:
        copy.start()
    for copy in label_copies:
        copy.wait()
    table = jnp.pad(costs[...], ((0, 16 - classes), (0, 128 - classes))) * (-0.5 * features)
    hi = table.astype(jnp.bfloat16)
    rest = table - hi.astype(jnp.float32)
    mid = rest.astype(jnp.bfloat16)
    low = (rest - mid.astype(jnp.float32)).astype(jnp.bfloat16)
    table = jnp.concatenate([hi, mid, low, jnp.zeros((80, 128), jnp.bfloat16)], axis=0)
    out = lax.dot_general(
        one_hot_rows(more_labels[...], 16), table, LAST, preferred_element_type=jnp.float32
    )
    label_rows[...] = out.astype(jnp.bfloat16)
    train_hot[...] = one_hot_rows(labels[...], 48)
    for copy in copies:
        copy.wait()


def train_kernel(tile, log_cols, source, row_pot, r0, r1, r2, r3, out, squares, buf, sems):
    rows, features = source.shape
    count, depth = rows // tile, buf.shape[0]

    def fetch(k):
        at = pl.ds(k * tile, tile)
        slot = lax.rem(k, depth)
        return pltpu.make_async_copy(source.at[at], buf.at[slot], sems.at[slot])

    for k in range(depth - 1):
        fetch(k).start()
    @pl.loop(0, count)
    def _(k):
        @pl.when(k + depth - 1 < count)
        def _():
            fetch(k + depth - 1).start()

        fetch(k).wait()
        for r in range(0, tile, 64):
            total = jnp.zeros((64, 128), jnp.float32)
            for c in range(features // 128):
                piece = buf[lax.rem(k, depth), pl.ds(r, 64), pl.ds(c * 128, 128)].astype(jnp.float32)
                total = total + piece * piece
            squares[pl.ds(pl.multiple_of(k * tile + r, 64), 64), :] = total
    ones = jnp.ones((SPLITS, 128), jnp.bfloat16)
    rest, norm = squares[...], 0.0
    for _ in range(3):
        part = rest.astype(jnp.bfloat16)
        rest = rest - part.astype(jnp.float32)
        norm = norm + lax.dot_general(ones, part, LAST, preferred_element_type=jnp.float32)
    total = (r0[...] + r1[...]) + (r2[...] + r3[...])
    pot = (row_pot[...] + (log_cols - jnp.log2(total))) * (1.0 / KAPPA)
    out[...] = pot + norm[0:1, :] * (1.0 / features)


def part_kernel(plan, count, row, tile, alpha, *refs):
    vals, (train, *given), results = refs[:count], refs[count : count + 3], refs[count + 3 :]
    first, last = given[0].dtype == jnp.bfloat16, alpha is not None
    if first:
        label_rows, train_hot = given
    else:
        before, sq_before = given
    scores, out = results[:2]
    sq = results[2] if last else out
    rows = train.shape[0]
    half = scores.shape[0] // 2
    pieces = len(plan[0][2])
    to = pl.ds(row, half * pieces)
    t = lax.axis_index("train")
    y, z = t // SIDE, t % SIDE

    def piece(part, r, n):
        place, start = part
        return vals[place][pl.ds(start + r, n), :]

    for h in range(pieces):
        for r in range(0, half, 128):
            at = pl.ds(row + h * half + r, 128)
            total = jnp.zeros((128, 128), jnp.float32) if first else sq_before[at, :]
            for _, _, parts in plan:
                value = piece(parts[h], r, 128).astype(jnp.float32)
                total = total + value * value
            if last:
                total = jnp.sum(total, axis=1, keepdims=True) * 0.5
                sq[pl.ds(h * half + r, 128), :] = jnp.broadcast_to(total, (128, 128))
            else:
                sq[at, :] = total

    @pl.loop(0, rows // tile, unroll=not last)
    def _(k):
        at = pl.ds(pl.multiple_of(k * tile, tile), tile)
        left, right = [], []
        for dy, dz, parts in plan:
            left.append(jnp.concatenate([piece(part, 0, half) for part in parts], axis=0))
            block = ((y + dy) % SIDE) * SIDE + (z + dz) % SIDE
            right.append(train[at, pl.ds(pl.multiple_of(block * 128, 128), 128)])
        if first:
            left.append(label_rows[to, :])
            right.append(train_hot[at, :])
        x = lax.dot_general(
            jnp.concatenate(left, axis=1),
            jnp.concatenate(right, axis=1),
            LAST,
            preferred_element_type=jnp.float32,
        )
        if not first:
            x = x + before[to, at]
        if last:
            x = (x - jnp.concatenate([sq[...]] * (tile // 128), axis=1)) * alpha
            peak = jnp.max(x, axis=0, keepdims=True)
            total = jnp.sum(jnp.exp2(x - peak), axis=0, keepdims=True)
            out[:, at] = peak + jnp.log2(total)
        scores[to, at] = x


def product_part(name, plan, row, tile, train, given, alpha=None):
    rows = train.shape[0]
    first, last = given[0].dtype == jnp.bfloat16, alpha is not None
    cols = given[0].shape[0]
    vals = []

    def place(array):
        for k, known in enumerate(vals):
            if known is array:
                return k
        vals.append(array)
        return len(vals) - 1

    plan = [(dy, dz, [(place(v), start) for v, start in parts]) for dy, dz, parts in plan]
    out = [pltpu.VMEM((cols, rows), jnp.float32)]
    out.append(shape_of((1, rows)) if last else shape_of((cols, 128)))
    given = given if first else [in_vmem(given[0]), given[1]]
    operands = [*vals, in_vmem(train), *given]
    depth = len(plan) * 128
    height = len(plan[0][2]) * cols // 2
    return pl.pallas_call(
        lambda *refs: part_kernel(plan, len(vals), row, tile, alpha, *refs),
        out_shape=tuple(out),
        in_specs=[VMEM] * len(operands),
        out_specs=(VMEM,) * len(out),
        scratch_shapes=[pltpu.VMEM((height, 128), jnp.float32)] if last else [],
        input_output_aliases={} if first else {len(operands) - 2: 0},
        compiler_params=params(SMALL),
        cost_estimate=pl.CostEstimate(
            flops=2 * height * rows * depth, bytes_accessed=0, transcendentals=0
        ),
        name=name,
    )(*operands)


def from_step(x, dy, dz):
    pairs = [
        (y * SIDE + z, ((y - dy) % SIDE) * SIDE + (z - dz) % SIDE)
        for y in range(SIDE)
        for z in range(SIDE)
    ]
    return lax.ppermute(x, "train", pairs)


def gather(x):
    h = x.shape[0] // 2
    low = lambda v, n: (v, n * h)
    cut = lambda v, n: v[n * h : (n + 1) * h]
    z1, z3 = from_step(x, 0, 1), from_step(x, 0, 3)
    y1, y3 = from_step(x, 1, 0), from_step(x, 3, 0)
    far = from_step(y1, 1, 2)
    both = lambda v: [low(v, 0), low(v, 1)]
    near = [(0, 0, both(x)), (0, 1, both(z1)), (0, 3, both(z3)), (1, 0, both(y1)), (3, 0, both(y3))]

    first = jnp.concatenate([cut(z1, 0), cut(z3, 0)], axis=0)
    second = jnp.concatenate([cut(y1, 1), cut(y3, 1)], axis=0)
    a1, a3 = from_step(first, 1, 0), from_step(first, 3, 0)
    b1, b3 = from_step(second, 0, 1), from_step(second, 0, 3)
    diagonal = [
        (dy, dz, [low(a, i), low(b, j)])
        for j, (dy, a) in enumerate(((1, a1), (3, a3)))
        for i, (dz, b) in enumerate(((1, b1), (3, b3)))
    ]
    diagonal.append((2, 2, both(far)))

    join = lambda *v: jnp.concatenate(v, axis=0)
    az = from_step(join(cut(z1, 0), cut(a1, 0), cut(a3, 0)), 0, 1)
    bz = from_step(join(cut(z3, 1), b3), 0, 3)
    by = from_step(join(cut(y1, 1), cut(b1, 0), cut(b3, 0)), 1, 0)
    ay = from_step(join(cut(y3, 0), a3), 3, 0)
    across = [(0, 2), (1, 2), (3, 2)]
    along = [(2, 0), (2, 1), (2, 3)]
    last_a = [(*d, [low(az, k)]) for k, d in enumerate(across)]
    last_a += [(*d, [low(ay, k)]) for k, d in enumerate(along)]
    last_b = [(*d, [low(bz, k)]) for k, d in enumerate(across)]
    last_b += [(*d, [low(by, k)]) for k, d in enumerate(along)]
    return near, diagonal, last_a, last_b


def kernel_kernel(log_cols, scores, l0, l1, l2, l3, kern, row_pot, peaks, col_log, peak_b, log_b):
    cols, rows = scores.shape
    pot = log_cols - logsum2([l0[...], l1[...], l2[...], l3[...]])
    row_pot[...] = pot
    block = 128

    @pl.loop(0, cols // block, unroll=4)
    def _(k):
        part = pl.ds(pl.multiple_of(k * block, block), block)
        peak = None
        for c in range(rows // 128):
            lane = pl.ds(c * 128, 128)
            x = scores[part, lane] + row_pot[:, lane]
            peak = x if peak is None else jnp.maximum(peak, x)
        peak = jnp.max(peak, axis=1, keepdims=True)
        peak = jnp.broadcast_to(peak, (block, 128))
        total = jnp.zeros((block, 128), jnp.float32)
        for c in range(rows // 128):
            lane = pl.ds(c * 128, 128)
            e = jnp.exp2((scores[part, lane] - peak) + row_pot[:, lane])
            total = total + e
            kern[part, lane] = e.astype(kern.dtype)
        total = jnp.sum(total, axis=1, keepdims=True)
        peak_b[part, :] = peak
        log_b[part, :] = peak + jnp.log2(total)

    for k in range(cols // 128):
        part = pl.ds(k * 128, 128)
        peaks[:, part] = turn(peak_b[part, :])
        turned = turn(log_b[part, :])
        for g in range(col_log.shape[0]):
            col_log[g, :, part] = turned


def first_rows_kernel(total_rows, kern, peaks, col_logs, weights, first_log, sums):
    logs = col_logs[...]
    peak = jnp.max(logs, axis=0)
    whole = peak + jnp.log2(jnp.sum(jnp.exp2(logs - peak[None]), axis=0))
    first_log[...] = whole
    v = jnp.exp2(peaks[...] - whole) * total_rows
    weights[...] = v
    out = jnp.dot(split_rows(v), kern[...], preferred_element_type=jnp.float32)
    sums[...] = jnp.sum(out, axis=0, keepdims=True)


def next_rows_kernel(total_rows, kern, weights, col_sums, sums):
    v = weights[...] * (total_rows / jnp.sum(col_sums[...], axis=0))
    out = jnp.dot(split_rows(v), kern[...], preferred_element_type=jnp.float32)
    sums[...] = jnp.sum(out, axis=0, keepdims=True)


def cols_kernel(total_cols, kern, weights, r0, r1, r2, r3, sums):
    u = total_cols / ((r0[...] + r1[...]) + (r2[...] + r3[...]))
    out = lax.dot_general(split_rows(u), kern[...], LAST, preferred_element_type=jnp.float32)
    out = jnp.sum(out, axis=0, keepdims=True) * weights[...]
    for g in range(sums.shape[0]):
        sums[g] = out


def other_chips(x):
    n = lax.axis_size("val")
    return [
        lax.ppermute(x, "val", [(i, (i + 2 * k) % n) for i in range(n)]) for k in range(1, n // 2)
    ]


def other_core(x):
    return lax.ppermute(x, "val", [(i, i ^ 1) for i in range(lax.axis_size("val"))])


def spread(x):
    return lax.all_to_all(x, "train", 0, 0)


def shards(train_embed, val_embed, train_labels, val_labels, label_cost):
    rows, features = train_embed.shape
    cols = val_embed.shape[0]
    groups = lax.axis_size("train")
    total_rows = float(rows * groups)
    total_cols = float(cols * lax.axis_size("val"))
    vec_r, vec_c = shape_of((1, rows)), shape_of((1, cols))

    near, diagonal, last_a, last_b = gather(val_embed)
    train, train_hot, label_rows = pl.pallas_call(
        lambda *refs: prepare_kernel(features, 512, *refs),
        out_shape=(
            pltpu.VMEM((rows, features), jnp.bfloat16),
            shape_of((rows, 128), jnp.bfloat16),
            shape_of((cols, 128), jnp.bfloat16),
        ),
        in_specs=[HBM] * 4,
        out_specs=(VMEM,) * 3,
        scratch_shapes=[
            pltpu.VMEM((1, rows), jnp.int32),
            pltpu.VMEM((1, cols), jnp.int32),
            pltpu.VMEM(label_cost.shape, jnp.float32),
            pltpu.SemaphoreType.DMA((rows // 512,)),
            pltpu.SemaphoreType.DMA((3,)),
        ],
        compiler_params=params(SMALL),
        name="prepare",
    )(
        in_hbm(label_cost),
        in_hbm(train_labels.reshape(1, rows)),
        in_hbm(val_labels.reshape(1, cols)),
        in_hbm(train_embed),
    )
    alpha = 2.0 * KAPPA / features
    given = product_part("product_near", near, 0, 1024, train, [label_rows, train_hot])
    scores, squares = product_part("product_diagonal", diagonal, 0, 1024, train, given)
    scores, log_a = product_part("product_a", last_a, 0, 1536, train, [scores, squares], alpha)
    scores, log_b = product_part(
        "product_b", last_b, cols // 2, 1536, train, [scores, squares], alpha
    )
    row_log = jnp.logaddexp2(log_a, log_b)

    both = jnp.logaddexp2(row_log, other_core(row_log))
    kern, row_pot, peaks, col_log = pl.pallas_call(
        lambda *refs: kernel_kernel(math.log2(total_cols), *refs),
        out_shape=(shape_of((cols, rows), jnp.bfloat16), vec_r, vec_c, shape_of((groups, 1, cols))),
        in_specs=[VMEM] * 5,
        out_specs=(VMEM,) * 4,
        scratch_shapes=[pltpu.VMEM((cols, 128), jnp.float32)] * 2,
        compiler_params=params(SMALL),
        name="kernel_matrix",
    )(scores, both, *other_chips(both))

    weights, first_log, sums = pl.pallas_call(
        lambda *refs: first_rows_kernel(total_rows, *refs),
        out_shape=(vec_c, vec_c, vec_r),
        in_specs=[VMEM] * 3,
        out_specs=(VMEM,) * 3,
        compiler_params=params(SMALL),
        name="first_rows",
    )(kern, peaks, spread(col_log))

    for sweep in range(2):
        both = sums + other_core(sums)
        others = other_chips(both)
        col_sums = pl.pallas_call(
            lambda *refs: cols_kernel(total_cols, *refs),
            out_shape=shape_of((groups, 1, cols)),
            in_specs=[VMEM] * 6,
            out_specs=VMEM,
            compiler_params=params(SMALL),
            name="columns",
        )(kern, weights, both, *others)
        col_sums = spread(col_sums)
        if sweep == 0:
            sums = pl.pallas_call(
                lambda *refs: next_rows_kernel(total_rows, *refs),
                out_shape=vec_r,
                in_specs=[VMEM] * 3,
                out_specs=VMEM,
                compiler_params=params(SMALL),
                name="rows",
            )(kern, weights, col_sums)

    train_potential = pl.pallas_call(
        lambda *refs: train_kernel(256, math.log2(total_cols), *refs),
        out_shape=vec_r,
        in_specs=[HBM] + [VMEM] * 5,
        out_specs=VMEM,
        scratch_shapes=[
            pltpu.VMEM((rows, 128), jnp.float32),
            pltpu.VMEM((7, 256, features), jnp.bfloat16),
            pltpu.SemaphoreType.DMA((7,)),
        ],
        compiler_params=params(14),
        name="train_potential",
    )(in_hbm(train_embed), row_pot, both, *others).reshape(rows)
    col_total = jnp.sum(col_sums, axis=0)
    val_potential = ((2.0 * math.log2(total_rows) - first_log) - jnp.log2(col_total)) / KAPPA
    return train_potential, val_potential.reshape(cols)


def solution(mesh):
    return jax.shard_map(
        shards,
        mesh=mesh,
        in_specs=(P("train", None), P("val", "train"), P("train"), P("val"), P()),
        out_specs=(P("train"), P("val")),
        check_vma=False,
    )
```

```python
import math

import jax
import jax.numpy as jnp
from jax import lax
from jax.experimental import pallas as pl
from jax.experimental.pallas import tpu as pltpu
from jax.sharding import PartitionSpec as P

EPS = 0.01
LOG2E = math.log2(math.e)
KAPPA = LOG2E / EPS
VMEM = pl.BlockSpec(memory_space=pltpu.VMEM)
HBM = pl.BlockSpec(memory_space=pltpu.HBM)
LAST = (((1,), (1,)), ((), ()))
SPLITS = 16
SMALL = 10
SIDE = 4


def params(mib):
    return pltpu.CompilerParams(vmem_limit_bytes=mib << 20)


def in_vmem(x):
    return pltpu.with_memory_space_constraint(x, pltpu.VMEM)


def in_hbm(x):
    return pltpu.with_memory_space_constraint(x, pltpu.HBM)


def shape_of(shape, dtype=jnp.float32):
    return jax.ShapeDtypeStruct(shape, dtype)


def split_rows(x):
    n = x.shape[1]
    row = lax.broadcasted_iota(jnp.int32, (SPLITS, n), 0)
    hi = x.astype(jnp.bfloat16).astype(jnp.float32)
    mid = (x - hi).astype(jnp.bfloat16).astype(jnp.float32)
    low = x - hi - mid
    parts = jnp.where(row == 0, hi, jnp.where(row == 1, mid, jnp.where(row == 2, low, 0.0)))
    return parts.astype(jnp.bfloat16)


def logsum2(rows):
    peak = rows[0]
    for r in rows[1:]:
        peak = jnp.maximum(peak, r)
    total = jnp.exp2(rows[0] - peak)
    for r in rows[1:]:
        total = total + jnp.exp2(r - peak)
    return peak + jnp.log2(total)


def lane_sums(x):
    ones = jnp.ones((SPLITS, 128), jnp.bfloat16)
    total = 0.0
    for _ in range(3):
        part = x.astype(jnp.bfloat16)
        x = x - part.astype(jnp.float32)
        total = total + lax.dot_general(ones, part, LAST, preferred_element_type=jnp.float32)
    return total[0:1, :]


def turn(block):
    r = lax.broadcasted_iota(jnp.int32, (128, 128), 0)
    c = lax.broadcasted_iota(jnp.int32, (128, 128), 1)
    return jnp.sum(jnp.where(r == c, block, 0.0), axis=0, keepdims=True)


def one_hot_rows(labels, slots):
    n = labels.shape[1]
    slot = lax.broadcasted_iota(jnp.int32, (128, n), 0)
    hot = ((slot % 16 == labels) & (slot < slots)).astype(jnp.float32)
    return jnp.transpose(hot).astype(jnp.bfloat16)


def prepare_kernel(
    features, tile, label_cost, train_labels, val_labels,
    source, train, train_hot, label_rows, labels, more_labels, costs, sems, label_sems,
):
    classes = label_cost.shape[0]
    label_copies = [
        pltpu.make_async_copy(train_labels, labels, label_sems.at[0]),
        pltpu.make_async_copy(val_labels, more_labels, label_sems.at[1]),
        pltpu.make_async_copy(label_cost, costs, label_sems.at[2]),
    ]
    spans = [pl.ds(k * tile, tile) for k in range(sems.shape[0])]
    copies = [
        pltpu.make_async_copy(source.at[at], train.at[at], sems.at[k]) for k, at in enumerate(spans)
    ]
    for copy in label_copies + copies:
        copy.start()
    for copy in label_copies:
        copy.wait()
    table = jnp.pad(costs[...], ((0, 16 - classes), (0, 128 - classes))) * (-0.5 * features)
    hi = table.astype(jnp.bfloat16)
    rest = table - hi.astype(jnp.float32)
    mid = rest.astype(jnp.bfloat16)
    low = (rest - mid.astype(jnp.float32)).astype(jnp.bfloat16)
    table = jnp.concatenate([hi, mid, low, jnp.zeros((80, 128), jnp.bfloat16)], axis=0)
    out = lax.dot_general(
        one_hot_rows(more_labels[...], 16), table, LAST, preferred_element_type=jnp.float32
    )
    label_rows[...] = out.astype(jnp.bfloat16)
    train_hot[...] = one_hot_rows(labels[...], 48)
    for copy in copies:
        copy.wait()


def train_kernel(tile, log_cols, source, row_pot, r0, r1, r2, r3, out, squares, buf, sems):
    rows, features = source.shape
    count, depth = rows // tile, buf.shape[0]

    def fetch(k):
        at = pl.ds(k * tile, tile)
        slot = lax.rem(k, depth)
        return pltpu.make_async_copy(source.at[at], buf.at[slot], sems.at[slot])

    for k in range(depth - 1):
        fetch(k).start()
    @pl.loop(0, count)
    def _(k):
        @pl.when(k + depth - 1 < count)
        def _():
            fetch(k + depth - 1).start()

        fetch(k).wait()
        for r in range(0, tile, 64):
            total = jnp.zeros((64, 128), jnp.float32)
            for c in range(features // 128):
                piece = buf[lax.rem(k, depth), pl.ds(r, 64), pl.ds(c * 128, 128)].astype(jnp.float32)
                total = total + piece * piece
            squares[pl.ds(pl.multiple_of(k * tile + r, 64), 64), :] = total
    norm = lane_sums(squares[...])
    total = (r0[...] + r1[...]) + (r2[...] + r3[...])
    pot = (row_pot[...] + (log_cols - jnp.log2(total))) * (1.0 / KAPPA)
    out[...] = pot + norm * (1.0 / features)


def part_kernel(plan, count, row, tile, alpha, early, *refs):
    vals, (train, *given), results = refs[:count], refs[count : count + 3], refs[count + 3 :]
    first, last = early is not None, alpha is not None
    if first:
        label_rows, train_hot = given
        source, *results = results
        more_train, sem = results[2:]
        span = pl.ds(early, train.shape[0] - early)
        copy = pltpu.make_async_copy(source.at[span], more_train.at[span], sem)
        copy.start()
    else:
        before, sq_before = given
    scores, out = results[:2]
    sq = results[2] if last else out
    rows = train.shape[0]
    half = scores.shape[0] // 2
    pieces = len(plan[0][2])
    to = pl.ds(row, half * pieces)
    t = lax.axis_index("train")
    y, z = t // SIDE, t % SIDE

    def piece(part, r, n):
        place, start = part
        return vals[place][pl.ds(start + r, n), :]

    for h in range(pieces):
        for r in range(0, half, 128):
            at = pl.ds(row + h * half + r, 128)
            total = jnp.zeros((128, 128), jnp.float32) if first else sq_before[at, :]
            for _, _, parts in plan:
                value = piece(parts[h], r, 128).astype(jnp.float32)
                total = total + value * value
            if last:
                total = jnp.sum(total, axis=1, keepdims=True) * 0.5
                sq[pl.ds(h * half + r, 128), :] = jnp.broadcast_to(total, (128, 128))
            else:
                sq[at, :] = total

    def work(k):
        at = pl.ds(k * tile if first else pl.multiple_of(k * tile, tile), tile)
        have = train
        if first and k * tile >= early:
            have = more_train
            if k * tile == early:
                copy.wait()
        left, right = [], []
        for dy, dz, parts in plan:
            left.append(jnp.concatenate([piece(part, 0, half) for part in parts], axis=0))
            block = ((y + dy) % SIDE) * SIDE + (z + dz) % SIDE
            right.append(have[at, pl.ds(pl.multiple_of(block * 128, 128), 128)])
        if first:
            left.append(label_rows[to, :])
            right.append(train_hot[at, :])
        x = lax.dot_general(
            jnp.concatenate(left, axis=1),
            jnp.concatenate(right, axis=1),
            LAST,
            preferred_element_type=jnp.float32,
        )
        if not first:
            x = x + before[to, at]
        if last:
            x = (x - jnp.concatenate([sq[...]] * (tile // 128), axis=1)) * alpha
            peak = jnp.max(x, axis=0, keepdims=True)
            total = jnp.sum(jnp.exp2(x - peak), axis=0, keepdims=True)
            out[:, at] = peak + jnp.log2(total)
        scores[to, at] = x

    if first:
        for k in range(rows // tile):
            work(k)
    else:
        pl.loop(0, rows // tile, unroll=not last)(work)


def product_part(name, plan, row, tile, train, given, alpha=None, source=None, early=None):
    rows = train.shape[0]
    first, last = source is not None, alpha is not None
    cols = given[0].shape[0]
    vals = []

    def place(array):
        for k, known in enumerate(vals):
            if known is array:
                return k
        vals.append(array)
        return len(vals) - 1

    plan = [(dy, dz, [(place(v), start) for v, start in parts]) for dy, dz, parts in plan]
    out = [pltpu.VMEM((cols, rows), jnp.float32)]
    out.append(shape_of((1, rows)) if last else shape_of((cols, 128)))
    given = given if first else [in_vmem(given[0]), given[1]]
    operands = [*vals, in_vmem(train), *given]
    specs = [VMEM] * len(operands)
    scratch, aliases = [], {len(operands) - 2: 0}
    if first:
        out.append(pltpu.VMEM(train.shape, train.dtype))
        operands.append(in_hbm(source))
        specs.append(HBM)
        scratch, aliases = [pltpu.SemaphoreType.DMA], {len(vals): 2}
    depth = len(plan) * 128
    height = len(plan[0][2]) * cols // 2
    return pl.pallas_call(
        lambda *refs: part_kernel(plan, len(vals), row, tile, alpha, early, *refs),
        out_shape=tuple(out),
        in_specs=specs,
        out_specs=(VMEM,) * len(out),
        scratch_shapes=[pltpu.VMEM((height, 128), jnp.float32)] if last else scratch,
        input_output_aliases=aliases,
        compiler_params=params(SMALL),
        cost_estimate=pl.CostEstimate(
            flops=2 * height * rows * depth, bytes_accessed=0, transcendentals=0
        ),
        name=name,
    )(*operands)


def from_step(x, dy, dz):
    pairs = [
        (y * SIDE + z, ((y - dy) % SIDE) * SIDE + (z - dz) % SIDE)
        for y in range(SIDE)
        for z in range(SIDE)
    ]
    return lax.ppermute(x, "train", pairs)


def gather(x):
    h = x.shape[0] // 2
    low = lambda v, n: (v, n * h)
    cut = lambda v, n: v[n * h : (n + 1) * h]
    z1, z3 = from_step(x, 0, 1), from_step(x, 0, 3)
    y1, y3 = from_step(x, 1, 0), from_step(x, 3, 0)
    far = from_step(y1, 1, 2)
    both = lambda v: [low(v, 0), low(v, 1)]
    near = [(0, 0, both(x)), (0, 1, both(z1)), (0, 3, both(z3)), (1, 0, both(y1)), (3, 0, both(y3))]

    first = jnp.concatenate([cut(z1, 0), cut(z3, 0)], axis=0)
    second = jnp.concatenate([cut(y1, 1), cut(y3, 1)], axis=0)
    a1, a3 = from_step(first, 1, 0), from_step(first, 3, 0)
    b1, b3 = from_step(second, 0, 1), from_step(second, 0, 3)
    diagonal = [
        (dy, dz, [low(a, i), low(b, j)])
        for j, (dy, a) in enumerate(((1, a1), (3, a3)))
        for i, (dz, b) in enumerate(((1, b1), (3, b3)))
    ]
    diagonal.append((2, 2, both(far)))

    join = lambda *v: jnp.concatenate(v, axis=0)
    az = from_step(join(cut(z1, 0), cut(a1, 0), cut(a3, 0)), 0, 1)
    bz = from_step(join(cut(z3, 1), b3), 0, 3)
    by = from_step(join(cut(y1, 1), cut(b1, 0), cut(b3, 0)), 1, 0)
    ay = from_step(join(cut(y3, 0), a3), 3, 0)
    across = [(0, 2), (1, 2), (3, 2)]
    along = [(2, 0), (2, 1), (2, 3)]
    last_a = [(*d, [low(az, k)]) for k, d in enumerate(across)]
    last_a += [(*d, [low(ay, k)]) for k, d in enumerate(along)]
    last_b = [(*d, [low(bz, k)]) for k, d in enumerate(across)]
    last_b += [(*d, [low(by, k)]) for k, d in enumerate(along)]
    return near, diagonal, last_a, last_b


def kernel_kernel(log_cols, scores, l0, l1, l2, l3, kern, row_pot, peaks, col_log, peak_b, log_b):
    cols, rows = scores.shape
    pot = log_cols - logsum2([l0[...], l1[...], l2[...], l3[...]])
    row_pot[...] = pot
    block = 128

    @pl.loop(0, cols // block, unroll=4)
    def _(k):
        part = pl.ds(pl.multiple_of(k * block, block), block)
        peak = None
        for c in range(rows // 128):
            lane = pl.ds(c * 128, 128)
            x = scores[part, lane] + row_pot[:, lane]
            peak = x if peak is None else jnp.maximum(peak, x)
        peak = jnp.max(peak, axis=1, keepdims=True)
        peak = jnp.broadcast_to(peak, (block, 128))
        total = jnp.zeros((block, 128), jnp.float32)
        for c in range(rows // 128):
            lane = pl.ds(c * 128, 128)
            e = jnp.exp2((scores[part, lane] - peak) + row_pot[:, lane])
            total = total + e
            kern[part, lane] = e.astype(kern.dtype)
        total = jnp.sum(total, axis=1, keepdims=True)
        peak_b[part, :] = peak
        log_b[part, :] = peak + jnp.log2(total)

    for k in range(cols // 128):
        part = pl.ds(k * 128, 128)
        peaks[:, part] = turn(peak_b[part, :])
        turned = turn(log_b[part, :])
        for g in range(col_log.shape[0]):
            col_log[g, :, part] = turned


def first_rows_kernel(total_rows, kern, peaks, col_logs, weights, first_log, sums):
    logs = col_logs[...]
    peak = jnp.max(logs, axis=0)
    whole = peak + jnp.log2(jnp.sum(jnp.exp2(logs - peak[None]), axis=0))
    first_log[...] = whole
    v = jnp.exp2(peaks[...] - whole) * total_rows
    weights[...] = v
    out = jnp.dot(split_rows(v), kern[...], preferred_element_type=jnp.float32)
    sums[...] = jnp.sum(out, axis=0, keepdims=True)


def next_rows_kernel(total_rows, kern, weights, col_sums, sums):
    v = weights[...] * (total_rows / jnp.sum(col_sums[...], axis=0))
    out = jnp.dot(split_rows(v), kern[...], preferred_element_type=jnp.float32)
    sums[...] = jnp.sum(out, axis=0, keepdims=True)


def cols_kernel(total_cols, kern, weights, r0, r1, r2, r3, sums, u):
    cols, rows = kern.shape
    u[...] = total_cols / ((r0[...] + r1[...]) + (r2[...] + r3[...]))
    block = 256
    for k in range(0, cols, block):
        part = pl.ds(k, block)
        total = jnp.zeros((block, 128), jnp.float32)
        for c in range(rows // 128):
            lane = pl.ds(c * 128, 128)
            total = total + kern[part, lane].astype(jnp.float32) * u[:, lane]
        out = lane_sums(total) * weights[:, part]
        for g in range(sums.shape[0]):
            sums[g, :, part] = out


def other_chips(x):
    n = lax.axis_size("val")
    return [
        lax.ppermute(x, "val", [(i, (i + 2 * k) % n) for i in range(n)]) for k in range(1, n // 2)
    ]


def other_core(x):
    return lax.ppermute(x, "val", [(i, i ^ 1) for i in range(lax.axis_size("val"))])


def spread(x):
    return lax.all_to_all(x, "train", 0, 0)


def shards(train_embed, val_embed, train_labels, val_labels, label_cost):
    rows, features = train_embed.shape
    cols = val_embed.shape[0]
    groups = lax.axis_size("train")
    total_rows = float(rows * groups)
    total_cols = float(cols * lax.axis_size("val"))
    vec_r, vec_c = shape_of((1, rows)), shape_of((1, cols))

    near, diagonal, last_a, last_b = gather(val_embed)
    early = rows // 3072 * 2048
    train, train_hot, label_rows = pl.pallas_call(
        lambda *refs: prepare_kernel(features, 512, *refs),
        out_shape=(
            pltpu.VMEM((rows, features), jnp.bfloat16),
            shape_of((rows, 128), jnp.bfloat16),
            shape_of((cols, 128), jnp.bfloat16),
        ),
        in_specs=[HBM] * 4,
        out_specs=(VMEM,) * 3,
        scratch_shapes=[
            pltpu.VMEM((1, rows), jnp.int32),
            pltpu.VMEM((1, cols), jnp.int32),
            pltpu.VMEM(label_cost.shape, jnp.float32),
            pltpu.SemaphoreType.DMA((early // 512,)),
            pltpu.SemaphoreType.DMA((3,)),
        ],
        compiler_params=params(SMALL),
        name="prepare",
    )(
        in_hbm(label_cost),
        in_hbm(train_labels.reshape(1, rows)),
        in_hbm(val_labels.reshape(1, cols)),
        in_hbm(train_embed),
    )
    alpha = 2.0 * KAPPA / features
    *given, train = product_part(
        "product_near",
        near,
        0,
        1024,
        train,
        [label_rows, train_hot],
        source=train_embed,
        early=early,
    )
    scores, squares = product_part("product_diagonal", diagonal, 0, 1024, train, given)
    scores, log_a = product_part("product_a", last_a, 0, 1536, train, [scores, squares], alpha)
    scores, log_b = product_part(
        "product_b", last_b, cols // 2, 1536, train, [scores, squares], alpha
    )
    row_log = jnp.logaddexp2(log_a, log_b)

    both = jnp.logaddexp2(row_log, other_core(row_log))
    kern, row_pot, peaks, col_log = pl.pallas_call(
        lambda *refs: kernel_kernel(math.log2(total_cols), *refs),
        out_shape=(shape_of((cols, rows), jnp.bfloat16), vec_r, vec_c, shape_of((groups, 1, cols))),
        in_specs=[VMEM] * 5,
        out_specs=(VMEM,) * 4,
        scratch_shapes=[pltpu.VMEM((cols, 128), jnp.float32)] * 2,
        compiler_params=params(SMALL),
        name="kernel_matrix",
    )(scores, both, *other_chips(both))

    weights, first_log, sums = pl.pallas_call(
        lambda *refs: first_rows_kernel(total_rows, *refs),
        out_shape=(vec_c, vec_c, vec_r),
        in_specs=[VMEM] * 3,
        out_specs=(VMEM,) * 3,
        compiler_params=params(SMALL),
        name="first_rows",
    )(kern, peaks, spread(col_log))

    for sweep in range(2):
        both = sums + other_core(sums)
        others = other_chips(both)
        col_sums = pl.pallas_call(
            lambda *refs: cols_kernel(total_cols, *refs),
            out_shape=shape_of((groups, 1, cols)),
            in_specs=[VMEM] * 6,
            out_specs=VMEM,
            scratch_shapes=[pltpu.VMEM((1, rows), jnp.float32)],
            compiler_params=params(SMALL),
            name="columns",
        )(kern, weights, both, *others)
        col_sums = spread(col_sums)
        if sweep == 0:
            sums = pl.pallas_call(
                lambda *refs: next_rows_kernel(total_rows, *refs),
                out_shape=vec_r,
                in_specs=[VMEM] * 3,
                out_specs=VMEM,
                compiler_params=params(SMALL),
                name="rows",
            )(kern, weights, col_sums)

    train_potential = pl.pallas_call(
        lambda *refs: train_kernel(256, math.log2(total_cols), *refs),
        out_shape=vec_r,
        in_specs=[HBM] + [VMEM] * 5,
        out_specs=VMEM,
        scratch_shapes=[
            pltpu.VMEM((rows, 128), jnp.float32),
            pltpu.VMEM((7, 256, features), jnp.bfloat16),
            pltpu.SemaphoreType.DMA((7,)),
        ],
        compiler_params=params(14),
        name="train_potential",
    )(in_hbm(train_embed), row_pot, both, *others).reshape(rows)
    col_total = jnp.sum(col_sums, axis=0)
    val_potential = ((2.0 * math.log2(total_rows) - first_log) - jnp.log2(col_total)) / KAPPA
    return train_potential, val_potential.reshape(cols)


def solution(mesh):
    return jax.shard_map(
        shards,
        mesh=mesh,
        in_specs=(P("train", None), P("val", "train"), P("train"), P("val"), P()),
        out_specs=(P("train"), P("val")),
        check_vma=False,
    )
```

```python
import math

import jax
import jax.numpy as jnp
from jax import lax
from jax.experimental import pallas as pl
from jax.experimental.pallas import tpu as pltpu
from jax.sharding import PartitionSpec as P

EPS = 0.01
LOG2E = math.log2(math.e)
KAPPA = LOG2E / EPS
VMEM = pl.BlockSpec(memory_space=pltpu.VMEM)
HBM = pl.BlockSpec(memory_space=pltpu.HBM)
LAST = (((1,), (1,)), ((), ()))
SPLITS = 16
SMALL = 10
SIDE = 4


def params(mib):
    return pltpu.CompilerParams(vmem_limit_bytes=mib << 20)


def in_vmem(x):
    return pltpu.with_memory_space_constraint(x, pltpu.VMEM)


def in_hbm(x):
    return pltpu.with_memory_space_constraint(x, pltpu.HBM)


def shape_of(shape, dtype=jnp.float32):
    return jax.ShapeDtypeStruct(shape, dtype)


def split_rows(x):
    n = x.shape[1]
    row = lax.broadcasted_iota(jnp.int32, (SPLITS, n), 0)
    hi = x.astype(jnp.bfloat16).astype(jnp.float32)
    mid = (x - hi).astype(jnp.bfloat16).astype(jnp.float32)
    low = x - hi - mid
    parts = jnp.where(row == 0, hi, jnp.where(row == 1, mid, jnp.where(row == 2, low, 0.0)))
    return parts.astype(jnp.bfloat16)


def logsum2(rows):
    peak = rows[0]
    for r in rows[1:]:
        peak = jnp.maximum(peak, r)
    total = jnp.exp2(rows[0] - peak)
    for r in rows[1:]:
        total = total + jnp.exp2(r - peak)
    return peak + jnp.log2(total)


def lane_sums(x):
    ones = jnp.ones((SPLITS, 128), jnp.bfloat16)
    total = 0.0
    for _ in range(3):
        part = x.astype(jnp.bfloat16)
        x = x - part.astype(jnp.float32)
        total = total + lax.dot_general(ones, part, LAST, preferred_element_type=jnp.float32)
    return total[0:1, :]


def turn(block):
    r = lax.broadcasted_iota(jnp.int32, (128, 128), 0)
    c = lax.broadcasted_iota(jnp.int32, (128, 128), 1)
    return jnp.sum(jnp.where(r == c, block, 0.0), axis=0, keepdims=True)


def one_hot_rows(labels, slots):
    n = labels.shape[1]
    slot = lax.broadcasted_iota(jnp.int32, (128, n), 0)
    hot = ((slot % 16 == labels) & (slot < slots)).astype(jnp.float32)
    return jnp.transpose(hot).astype(jnp.bfloat16)


def prepare_kernel(
    features, tile, label_cost, train_labels, val_labels,
    source, train, train_hot, label_rows, labels, more_labels, costs, sems, label_sems,
):
    classes = label_cost.shape[0]
    label_copies = [
        pltpu.make_async_copy(train_labels, labels, label_sems.at[0]),
        pltpu.make_async_copy(val_labels, more_labels, label_sems.at[1]),
        pltpu.make_async_copy(label_cost, costs, label_sems.at[2]),
    ]
    spans = [pl.ds(k * tile, tile) for k in range(sems.shape[0])]
    copies = [
        pltpu.make_async_copy(source.at[at], train.at[at], sems.at[k]) for k, at in enumerate(spans)
    ]
    for copy in label_copies + copies:
        copy.start()
    for copy in label_copies:
        copy.wait()
    table = jnp.pad(costs[...], ((0, 16 - classes), (0, 128 - classes))) * (-0.5 * features)
    hi = table.astype(jnp.bfloat16)
    rest = table - hi.astype(jnp.float32)
    mid = rest.astype(jnp.bfloat16)
    low = (rest - mid.astype(jnp.float32)).astype(jnp.bfloat16)
    table = jnp.concatenate([hi, mid, low, jnp.zeros((80, 128), jnp.bfloat16)], axis=0)
    out = lax.dot_general(
        one_hot_rows(more_labels[...], 16), table, LAST, preferred_element_type=jnp.float32
    )
    label_rows[...] = out.astype(jnp.bfloat16)
    train_hot[...] = one_hot_rows(labels[...], 48)
    for copy in copies:
        copy.wait()


def train_kernel(tile, log_cols, source, row_pot, r0, r1, r2, r3, out, squares, buf, sems):
    rows, features = source.shape
    count, depth = rows // tile, buf.shape[0]

    def fetch(k):
        at = pl.ds(k * tile, tile)
        slot = lax.rem(k, depth)
        return pltpu.make_async_copy(source.at[at], buf.at[slot], sems.at[slot])

    for k in range(depth - 1):
        fetch(k).start()
    @pl.loop(0, count)
    def _(k):
        @pl.when(k + depth - 1 < count)
        def _():
            fetch(k + depth - 1).start()

        fetch(k).wait()
        for r in range(0, tile, 64):
            total = jnp.zeros((64, 128), jnp.float32)
            for c in range(features // 128):
                piece = buf[lax.rem(k, depth), pl.ds(r, 64), pl.ds(c * 128, 128)].astype(jnp.float32)
                total = total + piece * piece
            squares[pl.ds(pl.multiple_of(k * tile + r, 64), 64), :] = total
    norm = lane_sums(squares[...])
    total = (r0[...] + r1[...]) + (r2[...] + r3[...])
    pot = (row_pot[...] + (log_cols - jnp.log2(total))) * (1.0 / KAPPA)
    out[...] = pot + norm * (1.0 / features)


def part_kernel(plan, count, row, tile, alpha, early, *refs):
    vals, (train, *given), results = refs[:count], refs[count : count + 3], refs[count + 3 :]
    first, last = early is not None, alpha is not None
    if first:
        label_rows, train_hot = given
        source, *results = results
        more_train, sem = results[2:]
        span = pl.ds(early, train.shape[0] - early)
        copy = pltpu.make_async_copy(source.at[span], more_train.at[span], sem)
        copy.start()
    else:
        before, sq_before = given
    scores, out = results[:2]
    sq = results[2] if last else out
    rows = train.shape[0]
    half = scores.shape[0] // 2
    pieces = len(plan[0][2])
    to = pl.ds(row, half * pieces)
    t = lax.axis_index("train")
    y, z = t // SIDE, t % SIDE

    def piece(part, r, n):
        place, start = part
        return vals[place][pl.ds(start + r, n), :]

    for h in range(pieces):
        for r in range(0, half, 128):
            at = pl.ds(row + h * half + r, 128)
            total = jnp.zeros((128, 128), jnp.float32) if first else sq_before[at, :]
            for _, _, parts in plan:
                value = piece(parts[h], r, 128).astype(jnp.float32)
                total = total + value * value
            if last:
                total = jnp.sum(total, axis=1, keepdims=True) * 0.5
                sq[pl.ds(h * half + r, 128), :] = jnp.broadcast_to(total, (128, 128))
            else:
                sq[at, :] = total

    def work(k):
        at = pl.ds(k * tile if first else pl.multiple_of(k * tile, tile), tile)
        have = train
        if first and k * tile >= early:
            have = more_train
            if k * tile == early:
                copy.wait()
        left, right = [], []
        for dy, dz, parts in plan:
            left.append(jnp.concatenate([piece(part, 0, half) for part in parts], axis=0))
            block = ((y + dy) % SIDE) * SIDE + (z + dz) % SIDE
            right.append(have[at, pl.ds(pl.multiple_of(block * 128, 128), 128)])
        if first:
            left.append(label_rows[to, :])
            right.append(train_hot[at, :])
        x = lax.dot_general(
            jnp.concatenate(left, axis=1),
            jnp.concatenate(right, axis=1),
            LAST,
            preferred_element_type=jnp.float32,
        )
        if not first:
            x = x + before[to, at]
        if last:
            x = (x - jnp.concatenate([sq[...]] * (tile // 128), axis=1)) * alpha
            peak = jnp.max(x, axis=0, keepdims=True)
            total = jnp.sum(jnp.exp2(x - peak), axis=0, keepdims=True)
            out[:, at] = peak + jnp.log2(total)
        scores[to, at] = x

    if first:
        for k in range(rows // tile):
            work(k)
    else:
        pl.loop(0, rows // tile, unroll=not last)(work)


def product_part(name, plan, row, tile, train, given, alpha=None, source=None, early=None):
    rows = train.shape[0]
    first, last = source is not None, alpha is not None
    cols = given[0].shape[0]
    vals = []

    def place(array):
        for k, known in enumerate(vals):
            if known is array:
                return k
        vals.append(array)
        return len(vals) - 1

    plan = [(dy, dz, [(place(v), start) for v, start in parts]) for dy, dz, parts in plan]
    out = [pltpu.VMEM((cols, rows), jnp.float32)]
    out.append(shape_of((1, rows)) if last else shape_of((cols, 128)))
    given = given if first else [in_vmem(given[0]), given[1]]
    operands = [*vals, in_vmem(train), *given]
    specs = [VMEM] * len(operands)
    scratch, aliases = [], {len(operands) - 2: 0}
    if first:
        out.append(pltpu.VMEM(train.shape, train.dtype))
        operands.append(in_hbm(source))
        specs.append(HBM)
        scratch, aliases = [pltpu.SemaphoreType.DMA], {len(vals): 2}
    depth = len(plan) * 128
    height = len(plan[0][2]) * cols // 2
    return pl.pallas_call(
        lambda *refs: part_kernel(plan, len(vals), row, tile, alpha, early, *refs),
        out_shape=tuple(out),
        in_specs=specs,
        out_specs=(VMEM,) * len(out),
        scratch_shapes=[pltpu.VMEM((height, 128), jnp.float32)] if last else scratch,
        input_output_aliases=aliases,
        compiler_params=params(SMALL),
        cost_estimate=pl.CostEstimate(
            flops=2 * height * rows * depth, bytes_accessed=0, transcendentals=0
        ),
        name=name,
    )(*operands)


def from_step(x, dy, dz):
    pairs = [
        (y * SIDE + z, ((y - dy) % SIDE) * SIDE + (z - dz) % SIDE)
        for y in range(SIDE)
        for z in range(SIDE)
    ]
    return lax.ppermute(x, "train", pairs)


def gather(x):
    h = x.shape[0] // 2
    low = lambda v, n: (v, n * h)
    cut = lambda v, n: v[n * h : (n + 1) * h]
    z1, z3 = from_step(x, 0, 1), from_step(x, 0, 3)
    y1, y3 = from_step(x, 1, 0), from_step(x, 3, 0)
    far = from_step(y3, 3, 2)
    both = lambda v: [low(v, 0), low(v, 1)]
    near = [(0, 0, both(x)), (0, 1, both(z1)), (0, 3, both(z3)), (1, 0, both(y1)), (3, 0, both(y3))]

    first = jnp.concatenate([cut(z1, 0), cut(z3, 0)], axis=0)
    second = jnp.concatenate([cut(y1, 1), cut(y3, 1)], axis=0)
    a1, a3 = from_step(first, 1, 0), from_step(first, 3, 0)
    b1, b3 = from_step(second, 0, 1), from_step(second, 0, 3)
    diagonal = [
        (dy, dz, [low(a, i), low(b, j)])
        for j, (dy, a) in enumerate(((1, a1), (3, a3)))
        for i, (dz, b) in enumerate(((1, b1), (3, b3)))
    ]
    diagonal.append((2, 2, both(far)))

    join = lambda *v: jnp.concatenate(v, axis=0)
    az = from_step(join(cut(z1, 0), cut(a1, 0), cut(a3, 0)), 0, 1)
    bz = from_step(join(cut(z3, 1), b3), 0, 3)
    by = from_step(join(cut(y1, 1), cut(b1, 0), cut(b3, 0)), 1, 0)
    ay = from_step(join(cut(y3, 0), a3), 3, 0)
    across = [(0, 2), (1, 2), (3, 2)]
    along = [(2, 0), (2, 1), (2, 3)]
    last_a = [(*d, [low(az, k)]) for k, d in enumerate(across)]
    last_a += [(*d, [low(ay, k)]) for k, d in enumerate(along)]
    last_b = [(*d, [low(bz, k)]) for k, d in enumerate(across)]
    last_b += [(*d, [low(by, k)]) for k, d in enumerate(along)]
    return near, diagonal, last_a, last_b


def kernel_kernel(log_cols, scores, l0, l1, l2, l3, kern, row_pot, peaks, col_log, peak_b, log_b):
    cols, rows = scores.shape
    pot = log_cols - logsum2([l0[...], l1[...], l2[...], l3[...]])
    row_pot[...] = pot
    block = 128

    @pl.loop(0, cols // block, unroll=4)
    def _(k):
        part = pl.ds(pl.multiple_of(k * block, block), block)
        peak = None
        for c in range(rows // 128):
            lane = pl.ds(c * 128, 128)
            x = scores[part, lane] + row_pot[:, lane]
            peak = x if peak is None else jnp.maximum(peak, x)
        peak = jnp.max(peak, axis=1, keepdims=True)
        peak = jnp.broadcast_to(peak, (block, 128))
        total = jnp.zeros((block, 128), jnp.float32)
        for c in range(rows // 128):
            lane = pl.ds(c * 128, 128)
            e = jnp.exp2((scores[part, lane] - peak) + row_pot[:, lane])
            total = total + e
            kern[part, lane] = e.astype(kern.dtype)
        total = jnp.sum(total, axis=1, keepdims=True)
        peak_b[part, :] = peak
        log_b[part, :] = peak + jnp.log2(total)

    for k in range(cols // 128):
        part = pl.ds(k * 128, 128)
        peaks[:, part] = turn(peak_b[part, :])
        turned = turn(log_b[part, :])
        for g in range(col_log.shape[0]):
            col_log[g, :, part] = turned


def first_rows_kernel(total_rows, kern, peaks, col_logs, weights, first_log, sums):
    logs = col_logs[...]
    peak = jnp.max(logs, axis=0)
    whole = peak + jnp.log2(jnp.sum(jnp.exp2(logs - peak[None]), axis=0))
    first_log[...] = whole
    v = jnp.exp2(peaks[...] - whole) * total_rows
    weights[...] = v
    out = jnp.dot(split_rows(v), kern[...], preferred_element_type=jnp.float32)
    sums[...] = jnp.sum(out, axis=0, keepdims=True)


def next_rows_kernel(total_rows, kern, weights, col_sums, sums):
    v = weights[...] * (total_rows / jnp.sum(col_sums[...], axis=0))
    out = jnp.dot(split_rows(v), kern[...], preferred_element_type=jnp.float32)
    sums[...] = jnp.sum(out, axis=0, keepdims=True)


def cols_kernel(total_cols, kern, weights, r0, r1, r2, r3, sums, u):
    cols, rows = kern.shape
    u[...] = total_cols / ((r0[...] + r1[...]) + (r2[...] + r3[...]))
    block = 256
    for k in range(0, cols, block):
        part = pl.ds(k, block)
        total = jnp.zeros((block, 128), jnp.float32)
        for c in range(rows // 128):
            lane = pl.ds(c * 128, 128)
            total = total + kern[part, lane].astype(jnp.float32) * u[:, lane]
        out = lane_sums(total) * weights[:, part]
        for g in range(sums.shape[0]):
            sums[g, :, part] = out


def other_chips(x):
    n = lax.axis_size("val")
    return [
        lax.ppermute(x, "val", [(i, (i + 2 * k) % n) for i in range(n)]) for k in range(1, n // 2)
    ]


def other_core(x):
    return lax.ppermute(x, "val", [(i, i ^ 1) for i in range(lax.axis_size("val"))])


def spread(x):
    return lax.all_to_all(x, "train", 0, 0)


def shards(train_embed, val_embed, train_labels, val_labels, label_cost):
    rows, features = train_embed.shape
    cols = val_embed.shape[0]
    groups = lax.axis_size("train")
    total_rows = float(rows * groups)
    total_cols = float(cols * lax.axis_size("val"))
    vec_r, vec_c = shape_of((1, rows)), shape_of((1, cols))

    near, diagonal, last_a, last_b = gather(val_embed)
    early = rows // 3072 * 2048
    train, train_hot, label_rows = pl.pallas_call(
        lambda *refs: prepare_kernel(features, 512, *refs),
        out_shape=(
            pltpu.VMEM((rows, features), jnp.bfloat16),
            shape_of((rows, 128), jnp.bfloat16),
            shape_of((cols, 128), jnp.bfloat16),
        ),
        in_specs=[HBM] * 4,
        out_specs=(VMEM,) * 3,
        scratch_shapes=[
            pltpu.VMEM((1, rows), jnp.int32),
            pltpu.VMEM((1, cols), jnp.int32),
            pltpu.VMEM(label_cost.shape, jnp.float32),
            pltpu.SemaphoreType.DMA((early // 512,)),
            pltpu.SemaphoreType.DMA((3,)),
        ],
        compiler_params=params(SMALL),
        name="prepare",
    )(
        in_hbm(label_cost),
        in_hbm(train_labels.reshape(1, rows)),
        in_hbm(val_labels.reshape(1, cols)),
        in_hbm(train_embed),
    )
    alpha = 2.0 * KAPPA / features
    *given, train = product_part(
        "product_near",
        near,
        0,
        1024,
        train,
        [label_rows, train_hot],
        source=train_embed,
        early=early,
    )
    scores, squares = product_part("product_diagonal", diagonal, 0, 1024, train, given)
    scores, log_a = product_part("product_a", last_a, 0, 1536, train, [scores, squares], alpha)
    scores, log_b = product_part(
        "product_b", last_b, cols // 2, 1536, train, [scores, squares], alpha
    )
    row_log = jnp.logaddexp2(log_a, log_b)

    both = jnp.logaddexp2(row_log, other_core(row_log))
    kern, row_pot, peaks, col_log = pl.pallas_call(
        lambda *refs: kernel_kernel(math.log2(total_cols), *refs),
        out_shape=(shape_of((cols, rows), jnp.bfloat16), vec_r, vec_c, shape_of((groups, 1, cols))),
        in_specs=[VMEM] * 5,
        out_specs=(VMEM,) * 4,
        scratch_shapes=[pltpu.VMEM((cols, 128), jnp.float32)] * 2,
        compiler_params=params(SMALL),
        name="kernel_matrix",
    )(scores, both, *other_chips(both))

    weights, first_log, sums = pl.pallas_call(
        lambda *refs: first_rows_kernel(total_rows, *refs),
        out_shape=(vec_c, vec_c, vec_r),
        in_specs=[VMEM] * 3,
        out_specs=(VMEM,) * 3,
        compiler_params=params(SMALL),
        name="first_rows",
    )(kern, peaks, spread(col_log))

    for sweep in range(2):
        both = sums + other_core(sums)
        others = other_chips(both)
        col_sums = pl.pallas_call(
            lambda *refs: cols_kernel(total_cols, *refs),
            out_shape=shape_of((groups, 1, cols)),
            in_specs=[VMEM] * 6,
            out_specs=VMEM,
            scratch_shapes=[pltpu.VMEM((1, rows), jnp.float32)],
            compiler_params=params(SMALL),
            name="columns",
        )(kern, weights, both, *others)
        col_sums = spread(col_sums)
        if sweep == 0:
            sums = pl.pallas_call(
                lambda *refs: next_rows_kernel(total_rows, *refs),
                out_shape=vec_r,
                in_specs=[VMEM] * 3,
                out_specs=VMEM,
                compiler_params=params(SMALL),
                name="rows",
            )(kern, weights, col_sums)

    train_potential = pl.pallas_call(
        lambda *refs: train_kernel(256, math.log2(total_cols), *refs),
        out_shape=vec_r,
        in_specs=[HBM] + [VMEM] * 5,
        out_specs=VMEM,
        scratch_shapes=[
            pltpu.VMEM((rows, 128), jnp.float32),
            pltpu.VMEM((7, 256, features), jnp.bfloat16),
            pltpu.SemaphoreType.DMA((7,)),
        ],
        compiler_params=params(14),
        name="train_potential",
    )(in_hbm(train_embed), row_pot, both, *others).reshape(rows)
    col_total = jnp.sum(col_sums, axis=0)
    val_potential = ((2.0 * math.log2(total_rows) - first_log) - jnp.log2(col_total)) / KAPPA
    return train_potential, val_potential.reshape(cols)


def solution(mesh):
    return jax.shard_map(
        shards,
        mesh=mesh,
        in_specs=(P("train", None), P("val", "train"), P("train"), P("val"), P()),
        out_specs=(P("train"), P("val")),
        check_vma=False,
    )
```

```python
import math

import jax
import jax.numpy as jnp
from jax import lax
from jax.experimental import pallas as pl
from jax.experimental.pallas import tpu as pltpu
from jax.sharding import PartitionSpec as P

EPS = 0.01
LOG2E = math.log2(math.e)
KAPPA = LOG2E / EPS
VMEM = pl.BlockSpec(memory_space=pltpu.VMEM)
HBM = pl.BlockSpec(memory_space=pltpu.HBM)
LAST = (((1,), (1,)), ((), ()))
SPLITS = 16
SMALL = 10
SIDE = 4


def params(mib):
    return pltpu.CompilerParams(vmem_limit_bytes=mib << 20)


def in_vmem(x):
    return pltpu.with_memory_space_constraint(x, pltpu.VMEM)


def in_hbm(x):
    return pltpu.with_memory_space_constraint(x, pltpu.HBM)


def shape_of(shape, dtype=jnp.float32):
    return jax.ShapeDtypeStruct(shape, dtype)


def split_rows(x):
    n = x.shape[1]
    row = lax.broadcasted_iota(jnp.int32, (SPLITS, n), 0)
    hi = x.astype(jnp.bfloat16).astype(jnp.float32)
    mid = (x - hi).astype(jnp.bfloat16).astype(jnp.float32)
    low = x - hi - mid
    parts = jnp.where(row == 0, hi, jnp.where(row == 1, mid, jnp.where(row == 2, low, 0.0)))
    return parts.astype(jnp.bfloat16)


def logsum2(rows):
    peak = rows[0]
    for r in rows[1:]:
        peak = jnp.maximum(peak, r)
    total = jnp.exp2(rows[0] - peak)
    for r in rows[1:]:
        total = total + jnp.exp2(r - peak)
    return peak + jnp.log2(total)


def lane_sums(x):
    ones = jnp.ones((SPLITS, 128), jnp.bfloat16)
    total = 0.0
    for _ in range(3):
        part = x.astype(jnp.bfloat16)
        x = x - part.astype(jnp.float32)
        total = total + lax.dot_general(ones, part, LAST, preferred_element_type=jnp.float32)
    return total[0:1, :]


def turn(block):
    r = lax.broadcasted_iota(jnp.int32, (128, 128), 0)
    c = lax.broadcasted_iota(jnp.int32, (128, 128), 1)
    return jnp.sum(jnp.where(r == c, block, 0.0), axis=0, keepdims=True)


def one_hot_rows(labels, slots):
    n = labels.shape[1]
    slot = lax.broadcasted_iota(jnp.int32, (128, n), 0)
    hot = ((slot % 16 == labels) & (slot < slots)).astype(jnp.float32)
    return jnp.transpose(hot).astype(jnp.bfloat16)


def prepare_kernel(
    features, tile, label_cost, train_labels, val_labels,
    source, train, train_hot, label_rows, labels, more_labels, costs, sems, label_sems,
):
    classes = label_cost.shape[0]
    label_copies = [
        pltpu.make_async_copy(train_labels, labels, label_sems.at[0]),
        pltpu.make_async_copy(val_labels, more_labels, label_sems.at[1]),
        pltpu.make_async_copy(label_cost, costs, label_sems.at[2]),
    ]
    spans = [pl.ds(k * tile, tile) for k in range(sems.shape[0])]
    copies = [
        pltpu.make_async_copy(source.at[at], train.at[at], sems.at[k]) for k, at in enumerate(spans)
    ]
    for copy in label_copies + copies:
        copy.start()
    for copy in label_copies:
        copy.wait()
    table = jnp.pad(costs[...], ((0, 16 - classes), (0, 128 - classes))) * (-0.5 * features)
    hi = table.astype(jnp.bfloat16)
    rest = table - hi.astype(jnp.float32)
    mid = rest.astype(jnp.bfloat16)
    low = (rest - mid.astype(jnp.float32)).astype(jnp.bfloat16)
    table = jnp.concatenate([hi, mid, low, jnp.zeros((80, 128), jnp.bfloat16)], axis=0)
    out = lax.dot_general(
        one_hot_rows(more_labels[...], 16), table, LAST, preferred_element_type=jnp.float32
    )
    label_rows[...] = out.astype(jnp.bfloat16)
    train_hot[...] = one_hot_rows(labels[...], 48)
    for copy in copies:
        copy.wait()


def train_kernel(tile, log_cols, source, row_pot, r0, r1, r2, r3, out, squares, buf, sems):
    rows, features = source.shape
    count, depth = rows // tile, buf.shape[0]

    def fetch(k):
        at = pl.ds(k * tile, tile)
        slot = lax.rem(k, depth)
        return pltpu.make_async_copy(source.at[at], buf.at[slot], sems.at[slot])

    for k in range(depth - 1):
        fetch(k).start()
    @pl.loop(0, count)
    def _(k):
        @pl.when(k + depth - 1 < count)
        def _():
            fetch(k + depth - 1).start()

        fetch(k).wait()
        for r in range(0, tile, 64):
            total = jnp.zeros((64, 128), jnp.float32)
            for c in range(features // 128):
                piece = buf[lax.rem(k, depth), pl.ds(r, 64), pl.ds(c * 128, 128)].astype(jnp.float32)
                total = total + piece * piece
            squares[pl.ds(pl.multiple_of(k * tile + r, 64), 64), :] = total
    norm = lane_sums(squares[...])
    total = (r0[...] + r1[...]) + (r2[...] + r3[...])
    pot = (row_pot[...] + (log_cols - jnp.log2(total))) * (1.0 / KAPPA)
    out[...] = pot + norm * (1.0 / features)


def part_kernel(plan, count, row, tile, alpha, early, *refs):
    vals, (train, *given), results = refs[:count], refs[count : count + 3], refs[count + 3 :]
    first, last = early is not None, alpha is not None
    if first:
        label_rows, train_hot = given
        source, *results = results
        more_train, sem = results[2:]
        span = pl.ds(early, train.shape[0] - early)
        copy = pltpu.make_async_copy(source.at[span], more_train.at[span], sem)
        copy.start()
    else:
        before, sq_before = given
    scores, out = results[:2]
    sq = results[2] if last else out
    rows = train.shape[0]
    half = scores.shape[0] // 2
    pieces = len(plan[0][2])
    to = pl.ds(row, half * pieces)
    t = lax.axis_index("train")
    y, z = t // SIDE, t % SIDE

    def piece(part, r, n):
        place, start = part
        return vals[place][pl.ds(start + r, n), :]

    for h in range(pieces):
        for r in range(0, half, 128):
            at = pl.ds(row + h * half + r, 128)
            total = jnp.zeros((128, 128), jnp.float32) if first else sq_before[at, :]
            for _, _, parts in plan:
                value = piece(parts[h], r, 128).astype(jnp.float32)
                total = total + value * value
            if last:
                total = jnp.sum(total, axis=1, keepdims=True) * 0.5
                sq[pl.ds(h * half + r, 128), :] = jnp.broadcast_to(total, (128, 128))
            else:
                sq[at, :] = total

    def work(k):
        at = pl.ds(k * tile if first else pl.multiple_of(k * tile, tile), tile)
        have = train
        if first and k * tile >= early:
            have = more_train
            if k * tile == early:
                copy.wait()
        left, right = [], []
        for dy, dz, parts in plan:
            left.append(jnp.concatenate([piece(part, 0, half) for part in parts], axis=0))
            block = ((y + dy) % SIDE) * SIDE + (z + dz) % SIDE
            right.append(have[at, pl.ds(pl.multiple_of(block * 128, 128), 128)])
        if first:
            left.append(label_rows[to, :])
            right.append(train_hot[at, :])
        x = lax.dot_general(
            jnp.concatenate(left, axis=1),
            jnp.concatenate(right, axis=1),
            LAST,
            preferred_element_type=jnp.float32,
        )
        if not first:
            x = x + before[to, at]
        if last:
            x = (x - jnp.concatenate([sq[...]] * (tile // 128), axis=1)) * alpha
            peak = jnp.max(x, axis=0, keepdims=True)
            total = jnp.sum(jnp.exp2(x - peak), axis=0, keepdims=True)
            out[:, at] = peak + jnp.log2(total)
        scores[to, at] = x

    if first:
        for k in range(rows // tile):
            work(k)
    else:
        pl.loop(0, rows // tile, unroll=not last)(work)


def product_part(name, plan, row, tile, train, given, alpha=None, source=None, early=None):
    rows = train.shape[0]
    first, last = source is not None, alpha is not None
    cols = given[0].shape[0]
    vals = []

    def place(array):
        for k, known in enumerate(vals):
            if known is array:
                return k
        vals.append(array)
        return len(vals) - 1

    plan = [(dy, dz, [(place(v), start) for v, start in parts]) for dy, dz, parts in plan]
    out = [pltpu.VMEM((cols, rows), jnp.float32)]
    out.append(shape_of((1, rows)) if last else shape_of((cols, 128)))
    given = given if first else [in_vmem(given[0]), given[1]]
    operands = [*vals, in_vmem(train), *given]
    specs = [VMEM] * len(operands)
    scratch, aliases = [], {len(operands) - 2: 0}
    if first:
        out.append(pltpu.VMEM(train.shape, train.dtype))
        operands.append(in_hbm(source))
        specs.append(HBM)
        scratch, aliases = [pltpu.SemaphoreType.DMA], {len(vals): 2}
    depth = len(plan) * 128
    height = len(plan[0][2]) * cols // 2
    return pl.pallas_call(
        lambda *refs: part_kernel(plan, len(vals), row, tile, alpha, early, *refs),
        out_shape=tuple(out),
        in_specs=specs,
        out_specs=(VMEM,) * len(out),
        scratch_shapes=[pltpu.VMEM((height, 128), jnp.float32)] if last else scratch,
        input_output_aliases=aliases,
        compiler_params=params(SMALL),
        cost_estimate=pl.CostEstimate(
            flops=2 * height * rows * depth, bytes_accessed=0, transcendentals=0
        ),
        name=name,
    )(*operands)


def from_step(x, dy, dz):
    pairs = [
        (y * SIDE + z, ((y - dy) % SIDE) * SIDE + (z - dz) % SIDE)
        for y in range(SIDE)
        for z in range(SIDE)
    ]
    return lax.ppermute(x, "train", pairs)


def gather(x):
    h = x.shape[0] // 2
    low = lambda v, n: (v, n * h)
    cut = lambda v, n: v[n * h : (n + 1) * h]
    z1, z3 = from_step(x, 0, 1), from_step(x, 0, 3)
    y1, y3 = from_step(x, 1, 0), from_step(x, 3, 0)
    far = from_step(y3, 3, 2)
    both = lambda v: [low(v, 0), low(v, 1)]
    near = [(0, 0, both(x)), (0, 1, both(z1)), (0, 3, both(z3)), (1, 0, both(y1)), (3, 0, both(y3))]

    first = jnp.concatenate([cut(z1, 0), cut(z3, 0)], axis=0)
    second = jnp.concatenate([cut(y1, 1), cut(y3, 1)], axis=0)
    a1, a3 = from_step(first, 1, 0), from_step(first, 3, 0)
    b1, b3 = from_step(second, 0, 1), from_step(second, 0, 3)
    diagonal = [
        (dy, dz, [low(a, i), low(b, j)])
        for j, (dy, a) in enumerate(((1, a1), (3, a3)))
        for i, (dz, b) in enumerate(((1, b1), (3, b3)))
    ]
    diagonal.append((2, 2, both(far)))

    join = lambda *v: jnp.concatenate(v, axis=0)
    az = from_step(join(cut(z1, 0), cut(a1, 0), cut(a3, 0)), 0, 1)
    bz = from_step(join(cut(z3, 1), b3), 0, 3)
    by = from_step(join(cut(y1, 1), cut(b1, 0), cut(b3, 0)), 1, 0)
    ay = from_step(join(cut(y3, 0), a3), 3, 0)
    across = [(0, 2), (1, 2), (3, 2)]
    along = [(2, 0), (2, 1), (2, 3)]
    last_a = [(*d, [low(az, k)]) for k, d in enumerate(across)]
    last_a += [(*d, [low(ay, k)]) for k, d in enumerate(along)]
    last_b = [(*d, [low(bz, k)]) for k, d in enumerate(across)]
    last_b += [(*d, [low(by, k)]) for k, d in enumerate(along)]
    return near, diagonal, last_a, last_b


def kernel_kernel(log_cols, scores, l0, l1, l2, l3, kern, row_pot, peaks, col_log, peak_b, log_b):
    cols, rows = scores.shape
    pot = log_cols - logsum2([l0[...], l1[...], l2[...], l3[...]])
    row_pot[...] = pot
    block = 128

    @pl.loop(0, cols // block, unroll=8)
    def _(k):
        part = pl.ds(pl.multiple_of(k * block, block), block)
        peak = None
        for c in range(rows // 128):
            lane = pl.ds(c * 128, 128)
            x = scores[part, lane] + row_pot[:, lane]
            peak = x if peak is None else jnp.maximum(peak, x)
        peak = jnp.max(peak, axis=1, keepdims=True)
        peak = jnp.broadcast_to(peak, (block, 128))
        total = jnp.zeros((block, 128), jnp.float32)
        for c in range(rows // 128):
            lane = pl.ds(c * 128, 128)
            e = jnp.exp2((scores[part, lane] - peak) + row_pot[:, lane])
            total = total + e
            kern[part, lane] = e.astype(kern.dtype)
        total = jnp.sum(total, axis=1, keepdims=True)
        peak_b[part, :] = peak
        log_b[part, :] = peak + jnp.log2(total)

    for k in range(cols // 128):
        part = pl.ds(k * 128, 128)
        peaks[:, part] = turn(peak_b[part, :])
        turned = turn(log_b[part, :])
        for g in range(col_log.shape[0]):
            col_log[g, :, part] = turned


def first_rows_kernel(total_rows, kern, peaks, col_logs, weights, first_log, sums):
    logs = col_logs[...]
    peak = jnp.max(logs, axis=0)
    whole = peak + jnp.log2(jnp.sum(jnp.exp2(logs - peak[None]), axis=0))
    first_log[...] = whole
    v = jnp.exp2(peaks[...] - whole) * total_rows
    weights[...] = v
    out = jnp.dot(split_rows(v), kern[...], preferred_element_type=jnp.float32)
    sums[...] = jnp.sum(out, axis=0, keepdims=True)


def next_rows_kernel(total_rows, kern, weights, col_sums, sums):
    v = weights[...] * (total_rows / jnp.sum(col_sums[...], axis=0))
    out = jnp.dot(split_rows(v), kern[...], preferred_element_type=jnp.float32)
    sums[...] = jnp.sum(out, axis=0, keepdims=True)


def cols_kernel(total_cols, kern, weights, r0, r1, r2, r3, sums, u):
    cols, rows = kern.shape
    u[...] = total_cols / ((r0[...] + r1[...]) + (r2[...] + r3[...]))
    block = 256
    for k in range(0, cols, block):
        part = pl.ds(k, block)
        total = jnp.zeros((block, 128), jnp.float32)
        for c in range(rows // 128):
            lane = pl.ds(c * 128, 128)
            total = total + kern[part, lane].astype(jnp.float32) * u[:, lane]
        out = lane_sums(total) * weights[:, part]
        for g in range(sums.shape[0]):
            sums[g, :, part] = out


def other_chips(x):
    n = lax.axis_size("val")
    return [
        lax.ppermute(x, "val", [(i, (i + 2 * k) % n) for i in range(n)]) for k in range(1, n // 2)
    ]


def other_core(x):
    return lax.ppermute(x, "val", [(i, i ^ 1) for i in range(lax.axis_size("val"))])


def spread(x):
    return lax.all_to_all(x, "train", 0, 0)


def shards(train_embed, val_embed, train_labels, val_labels, label_cost):
    rows, features = train_embed.shape
    cols = val_embed.shape[0]
    groups = lax.axis_size("train")
    total_rows = float(rows * groups)
    total_cols = float(cols * lax.axis_size("val"))
    vec_r, vec_c = shape_of((1, rows)), shape_of((1, cols))

    near, diagonal, last_a, last_b = gather(val_embed)
    early = rows // 3072 * 2048
    train, train_hot, label_rows = pl.pallas_call(
        lambda *refs: prepare_kernel(features, 512, *refs),
        out_shape=(
            pltpu.VMEM((rows, features), jnp.bfloat16),
            shape_of((rows, 128), jnp.bfloat16),
            shape_of((cols, 128), jnp.bfloat16),
        ),
        in_specs=[HBM] * 4,
        out_specs=(VMEM,) * 3,
        scratch_shapes=[
            pltpu.VMEM((1, rows), jnp.int32),
            pltpu.VMEM((1, cols), jnp.int32),
            pltpu.VMEM(label_cost.shape, jnp.float32),
            pltpu.SemaphoreType.DMA((early // 512,)),
            pltpu.SemaphoreType.DMA((3,)),
        ],
        compiler_params=params(SMALL),
        name="prepare",
    )(
        in_hbm(label_cost),
        in_hbm(train_labels.reshape(1, rows)),
        in_hbm(val_labels.reshape(1, cols)),
        in_hbm(train_embed),
    )
    alpha = 2.0 * KAPPA / features
    *given, train = product_part(
        "product_near",
        near,
        0,
        1024,
        train,
        [label_rows, train_hot],
        source=train_embed,
        early=early,
    )
    scores, squares = product_part("product_diagonal", diagonal, 0, 1024, train, given)
    scores, log_a = product_part("product_a", last_a, 0, 1536, train, [scores, squares], alpha)
    scores, log_b = product_part(
        "product_b", last_b, cols // 2, 1536, train, [scores, squares], alpha
    )
    row_log = jnp.logaddexp2(log_a, log_b)

    both = jnp.logaddexp2(row_log, other_core(row_log))
    kern, row_pot, peaks, col_log = pl.pallas_call(
        lambda *refs: kernel_kernel(math.log2(total_cols), *refs),
        out_shape=(shape_of((cols, rows), jnp.bfloat16), vec_r, vec_c, shape_of((groups, 1, cols))),
        in_specs=[VMEM] * 5,
        out_specs=(VMEM,) * 4,
        scratch_shapes=[pltpu.VMEM((cols, 128), jnp.float32)] * 2,
        compiler_params=params(SMALL),
        name="kernel_matrix",
    )(scores, both, *other_chips(both))

    weights, first_log, sums = pl.pallas_call(
        lambda *refs: first_rows_kernel(total_rows, *refs),
        out_shape=(vec_c, vec_c, vec_r),
        in_specs=[VMEM] * 3,
        out_specs=(VMEM,) * 3,
        compiler_params=params(SMALL),
        name="first_rows",
    )(kern, peaks, spread(col_log))

    for sweep in range(2):
        both = sums + other_core(sums)
        others = other_chips(both)
        col_sums = pl.pallas_call(
            lambda *refs: cols_kernel(total_cols, *refs),
            out_shape=shape_of((groups, 1, cols)),
            in_specs=[VMEM] * 6,
            out_specs=VMEM,
            scratch_shapes=[pltpu.VMEM((1, rows), jnp.float32)],
            compiler_params=params(SMALL),
            name="columns",
        )(kern, weights, both, *others)
        col_sums = spread(col_sums)
        if sweep == 0:
            sums = pl.pallas_call(
                lambda *refs: next_rows_kernel(total_rows, *refs),
                out_shape=vec_r,
                in_specs=[VMEM] * 3,
                out_specs=VMEM,
                compiler_params=params(SMALL),
                name="rows",
            )(kern, weights, col_sums)

    train_potential = pl.pallas_call(
        lambda *refs: train_kernel(256, math.log2(total_cols), *refs),
        out_shape=vec_r,
        in_specs=[HBM] + [VMEM] * 5,
        out_specs=VMEM,
        scratch_shapes=[
            pltpu.VMEM((rows, 128), jnp.float32),
            pltpu.VMEM((7, 256, features), jnp.bfloat16),
            pltpu.SemaphoreType.DMA((7,)),
        ],
        compiler_params=params(14),
        name="train_potential",
    )(in_hbm(train_embed), row_pot, both, *others).reshape(rows)
    col_total = jnp.sum(col_sums, axis=0)
    val_potential = ((2.0 * math.log2(total_rows) - first_log) - jnp.log2(col_total)) / KAPPA
    return train_potential, val_potential.reshape(cols)


def solution(mesh):
    return jax.shard_map(
        shards,
        mesh=mesh,
        in_specs=(P("train", None), P("val", "train"), P("train"), P("val"), P()),
        out_specs=(P("train"), P("val")),
        check_vma=False,
    )
```
